128 devices in a mesh: row: 8 (over y, core), col: 16 (over x, z).
Axes of the slice: x: 4, y: 4, z: 4, core: 2. Of those that a mesh axis runs over, the one named last changes fastest.
Arguments:
- tokens: bfloat16 [1024, 16384], P('col', 'row'), may hold values from -6 to 6
- w_qkv: bfloat16 [2, 3, 1024, 1024], P(None, None, 'col', 'row'), may hold values from -0.1875 to 0.1875
- bias_qv: float32 [2, 2, 1024], P(None, None, 'col'), may hold values from -3 to 3
- w_out: bfloat16 [2, 1024, 1024], P(None, 'col', 'row'), may hold values from -3.5 to 3.5
- bias_out: float32 [2, 1024], P(None, 'col'), may hold values from -2 to 2
- gain_attn: float32 [2, 1024], P(None, 'col'), may hold values from 0.1 to 1.9
- shift_attn: float32 [2, 1024], P(None, 'col'), may hold values from -2 to 2
- w_up: bfloat16 [2, 4096, 1024], P(None, 'col', 'row'), may hold values from -0.1875 to 0.1875
- bias_up: float32 [2, 4096], P(None, 'col'), may hold values from -3 to 3
- w_down: bfloat16 [2, 1024, 4096], P(None, 'col', 'row'), may hold values from -0.125 to 0.125
- bias_down: float32 [2, 1024], P(None, 'col'), may hold values from -2 to 2
- gain_ffn: float32 [2, 1024], P(None, 'col'), may hold values from 0.1 to 1.9
- shift_ffn: float32 [2, 1024], P(None, 'col'), may hold values from -2 to 2
- cotangent: bfloat16 [1024, 16384], P('col', 'row'), may hold values from -6 to 6
Outputs:
- output: bfloat16 [1024, 16384], P('col', 'row')
- grad_tokens: float32 [1024, 16384], P('col', 'row')
- grad_w_qkv: float32 [2, 3, 1024, 1024], P(None, None, 'col', 'row')
- grad_bias_qv: float32 [2, 2, 1024], P(None, None, 'col')
- grad_w_out: float32 [2, 1024, 1024], P(None, 'col', 'row')
- grad_bias_out: float32 [2, 1024], P(None, 'col')
- grad_gain_attn: float32 [2, 1024], P(None, 'col')
- grad_shift_attn: float32 [2, 1024], P(None, 'col')
- grad_w_up: float32 [2, 4096, 1024], P(None, 'col', 'row')
- grad_bias_up: float32 [2, 4096], P(None, 'col')
- grad_w_down: float32 [2, 1024, 4096], P(None, 'col', 'row')
- grad_bias_down: float32 [2, 1024], P(None, 'col')
- grad_gain_ffn: float32 [2, 1024], P(None, 'col')
- grad_shift_ffn: float32 [2, 1024], P(None, 'col')
The draws below stay inside these ranges and needn't reach their ends.
All inputs are finite; a program needn't handle non-finite values.
Results may differ from the reference program's by a relative error of at most 0.04.
Values may be sent and summed in bfloat16 or wider, within the bound.
No kernel may reach another device: no remote copies, remote signals or barrier semaphores. Data moves between devices by JAX's collectives and lax.ppermute only.
A program may use at most 256 MiB of HBM per device.

```python
import jax
import jax.numpy as jnp
from jax import lax

HEADS = 16
HEAD = 64
D = 1024
FF = 4096
LAYERS = 2
SEQ_LEN = 1024
SEQS = 16
TOKENS = 16384


def block_levels(key, extent, split, least, top_value):
    level = 1.0
    for dim, shards_of in split:
        heights = jax.random.uniform(jax.random.fold_in(jax.random.fold_in(key, 6), dim), (shards_of,), jnp.float32, least / len(split), top_value / len(split))
        level = level * jnp.repeat(jnp.exp(heights), extent[dim] // shards_of).reshape((-1,) + (1,) * (len(extent) - 1 - dim))
    return level


def normal_values(rng, shape, spread, bound, split=(), held_as=jnp.bfloat16):
    values = jax.random.normal(rng, shape, jnp.float32) * spread
    if len(split) > 0:
        values = block_levels(rng, shape, split, -0.22, 0.18) * values
    return jnp.clip(values, min=-bound, max=bound).astype(held_as)


def setup_inputs(seed: int = 0) -> dict:
    splits = jax.random.split(jax.random.key(seed), 15)
    tokens = normal_values(splits[0], (D, TOKENS), 1.0, 6.0, ((0, 16), (1, 8)))
    w_qkv = normal_values(splits[1], (LAYERS, 3, D, D), D ** -0.5, 0.1875, ((2, 16), (3, 8)))
    bias_qv = normal_values(splits[2], (LAYERS, 2, D), 0.5, 3.0, ((2, 16),), jnp.float32)
    w_out = normal_values(splits[3], (LAYERS, D, D), (3 * D // SEQ_LEN) ** -0.5, 3.5, ((1, 16), (2, 8)))
    bias_out = normal_values(splits[4], (LAYERS, D), 0.3, 2.0, ((1, 16),), jnp.float32)
    gain_attn = jnp.clip(1.0 + 0.18 * jax.random.normal(splits[5], (LAYERS, D), jnp.float32), 0.1, 1.9)
    shift_attn = normal_values(splits[6], (LAYERS, D), 0.3, 2.0, ((1, 16),), jnp.float32)
    w_up = normal_values(splits[7], (LAYERS, FF, D), D ** -0.5, 0.1875, ((1, 16), (2, 8)))
    bias_up = normal_values(splits[8], (LAYERS, FF), 0.5, 3.0, ((1, 16),), jnp.float32)
    w_down = normal_values(splits[9], (LAYERS, D, FF), (FF // 2) ** -0.5, 0.125, ((1, 16), (2, 8)))
    bias_down = normal_values(splits[10], (LAYERS, D), 0.3, 2.0, ((1, 16),), jnp.float32)
    gain_ffn = jnp.clip(1.0 + 0.18 * jax.random.normal(splits[11], (LAYERS, D), jnp.float32), 0.1, 1.9)
    shift_ffn = normal_values(splits[12], (LAYERS, D), 0.3, 2.0, ((1, 16),), jnp.float32)
    cotangent = normal_values(splits[13], (D, TOKENS), 1.0, 6.0, ((0, 16), (1, 8)))
    return dict(tokens=tokens, w_qkv=w_qkv, bias_qv=bias_qv, w_out=w_out, bias_out=bias_out, gain_attn=gain_attn, shift_attn=shift_attn, w_up=w_up, bias_up=bias_up, w_down=w_down, bias_down=bias_down, gain_ffn=gain_ffn, shift_ffn=shift_ffn, cotangent=cotangent)


highest = lax.Precision.HIGHEST
epsilon = 1e-05

@jax.custom_vjp
def low(v):
    return lax.optimization_barrier(v.astype(jnp.bfloat16)).astype(jnp.float32)

@jax.custom_vjp
def low_back(v):
    return v

def low_keep(v):
    return (low(v), None)

def low_pass(kept, grad):
    return (grad,)

def back_keep(v):
    return (v, None)

def back_low(kept, grad):
    return (low(grad),)
low.defvjp(low_keep, low_pass)
low_back.defvjp(back_keep, back_low)

def both_ways(values):
    return low(low_back(values))

def layer_norm(summed, gain, shift):
    centre = lax.optimization_barrier(jnp.mean(summed, axis=-1, keepdims=True))
    centred = summed - centre
    variance = lax.optimization_barrier(jnp.mean(centred * centred, axis=-1, keepdims=True))
    return centred * lax.rsqrt(variance + epsilon) * gain + shift

def attend(blocks):
    queries, key_part, value_part = blocks
    scores = jnp.einsum('qhd,khd->hqk', queries, key_part, precision=highest) * HEAD ** (-0.5)
    scores = low_back(scores)
    probs_low = low(jax.nn.softmax(scores, axis=-1))
    return jnp.einsum('hqk,khd->qhd', probs_low, value_part, precision=highest)

def encoder(stream, w_qkv, bias_qv, w_out, bias_out, gain_attn, shift_attn, w_up, bias_up, w_down, bias_down, gain_ffn, shift_ffn):
    seen = low(stream)
    bias_three = jnp.stack([bias_qv[0], jnp.zeros_like(bias_qv[0]), bias_qv[1]])
    qkv = jnp.einsum('td,dje->tje', seen, w_qkv, precision=highest) + bias_three
    qkv = both_ways(qkv)
    shaped = qkv.reshape(SEQS, SEQ_LEN, 3, HEADS, HEAD)
    blended = lax.map(jax.checkpoint(attend), (shaped[:, :, 0], shaped[:, :, 1], shaped[:, :, 2]))
    blended = both_ways(blended.reshape(TOKENS, D))
    attn_out = low_back(jnp.dot(blended, w_out, precision=highest) + bias_out)
    first_out = layer_norm(stream + attn_out, gain_attn, shift_attn)
    upper_pre = low_back(jnp.dot(low(first_out), w_up, precision=highest) + bias_up)
    active = low(jax.nn.gelu(upper_pre, approximate=False))
    lower_out = low_back(jnp.dot(active, w_down, precision=highest) + bias_down)
    return layer_norm(first_out + lower_out, gain_ffn, shift_ffn)

def forward(stream, *tensors):
    for layer_idx in range(LAYERS):
        stream = encoder(stream, *[tensor[layer_idx] for tensor in tensors])
    return stream

def reference(tokens, w_qkv, bias_qv, w_out, bias_out, gain_attn, shift_attn, w_up, bias_up, w_down, bias_down, gain_ffn, shift_ffn, cotangent):
    plain = [tensor.astype(jnp.float32) for tensor in (w_qkv, bias_qv, w_out, bias_out, gain_attn, shift_attn, w_up, bias_up, w_down, bias_down, gain_ffn, shift_ffn)]
    plain[0] = jnp.transpose(plain[0], (0, 3, 1, 2))
    plain[2] = jnp.transpose(plain[2], (0, 2, 1))
    plain[6] = jnp.transpose(plain[6], (0, 2, 1))
    plain[8] = jnp.transpose(plain[8], (0, 2, 1))
    result, pullback = jax.vjp(forward, tokens.astype(jnp.float32).T, *plain)
    grads = pullback(cotangent.astype(jnp.float32).T)
    return (result.T.astype(jnp.bfloat16), grads[0].T, jnp.transpose(grads[1], (0, 2, 3, 1)), grads[2], jnp.transpose(grads[3], (0, 2, 1)), grads[4], grads[5], grads[6], jnp.transpose(grads[7], (0, 2, 1)), grads[8], jnp.transpose(grads[9], (0, 2, 1)), grads[10], grads[11], grads[12])
```

```python
import jax
import jax.numpy as jnp
from jax import lax
from jax.sharding import Mesh, PartitionSpec as P

HEAD = 64
D = 1024
LAYERS = 2
SEQ_LEN = 1024
epsilon = 1e-05

CORE = "k"
Y = ("y",)
X = ("xh", "xl")
Z = ("zh", "zl")
COL = X + Z
CHIPS = Y + COL
SEQ = ("xl", "zh", "zl")
bf16 = jnp.bfloat16
f32 = jnp.float32


def dot(a, b, ca, cb):
    return lax.dot_general(a, b, (((ca,), (cb,)), ((), ())), preferred_element_type=f32)


def core_gather(values):
    return lax.all_gather(values, CORE, axis=1, tiled=True)


def core_reduce(part):
    me = lax.axis_index(CORE)
    halves = part.reshape(part.shape[0], 2, part.shape[1] // 2)
    keep = jnp.where(me == 0, halves[:, 0], halves[:, 1])
    send = jnp.where(me == 0, halves[:, 1], halves[:, 0]).astype(bf16)
    return keep + lax.ppermute(send, CORE, [(0, 1), (1, 0)]).astype(f32)


def trade(values):
    return lax.ppermute(values, (CORE, "zh"), [(0, 0), (1, 2), (2, 1), (3, 3)])


def pick(values, index, dim):
    return lax.dynamic_index_in_dim(values, index, dim, keepdims=False)


def scatter_axis(chunk_of, axes):
    me = lax.axis_index(axes)
    total = chunk_of(me).astype(f32)
    for shift in (1, 3, 2):
        sent = chunk_of((me + shift) % 4)
        total += lax.ppermute(sent, axes, [(i, (i + shift) % 4) for i in range(4)]).astype(f32)
    return total


def sum_axis(values, axes):
    total = values
    for shift in (1, 3, 2):
        total += lax.ppermute(values, axes, [(i, (i + shift) % 4) for i in range(4)])
    return total


def reduce_down(g):
    g = g.reshape(4, 4, 64, 4, 512)
    g = scatter_axis(lambda i: pick(g, i, 3), Y).astype(bf16)
    h = scatter_axis(lambda i: pick(g, i, 1), Z).astype(bf16)
    return scatter_axis(lambda i: pick(h, i, 0), X)


def reduce_up(g):
    g = g.reshape(4, 512, 1024)
    h = scatter_axis(lambda i: pick(g, i, 0), X).astype(bf16)
    h = h.reshape(512, 4, 256)
    q = scatter_axis(lambda i: pick(h, i, 1), Y).astype(bf16)
    q = q.reshape(2, 256, 2, 128).transpose(2, 0, 1, 3).reshape(4, 256, 128)
    return scatter_axis(lambda i: pick(q, i, 0), Z)


def reduce_qo(g_qkv, g_out):
    g_qkv = g_qkv.reshape(3, 4, 2, 64, 4, 2, 128)
    g_out = g_out.reshape(4, 4, 64, 4, 128)

    def chunk(i):
        a = pick(pick(g_qkv, i // 2, 5), i % 2, 2)
        b = pick(g_out, i, 1)
        return jnp.concatenate([a, b[None]], axis=0)

    h = scatter_axis(chunk, Z).astype(bf16)
    h2 = scatter_axis(lambda i: pick(h, i, 1), X).astype(bf16)
    return scatter_axis(lambda i: pick(h2, i, 2), Y)


def norm_forward(summed, gain, shift):
    centre = jnp.mean(summed, axis=0, keepdims=True)
    centred = summed - centre
    variance = jnp.mean(centred * centred, axis=0, keepdims=True)
    scaled = lax.rsqrt(variance + epsilon)
    normed = centred * scaled
    return normed * gain[:, None] + shift[:, None], normed, scaled


def norm_backward(incoming, normed, scaled, gain):
    grad_norm = incoming * gain[:, None]
    plain = jnp.mean(grad_norm, axis=0, keepdims=True)
    cross = jnp.mean(grad_norm * normed, axis=0, keepdims=True)
    return scaled * (grad_norm - plain - normed * cross)


def to_heads(values, kinds):
    v = values.reshape(kinds, 4, 128, 2, 128).transpose(3, 1, 0, 2, 4)
    v = v.reshape(8, kinds * 128, 128)
    v = lax.all_to_all(v, SEQ, 0, 2, tiled=True)
    return v.reshape(kinds, 2, HEAD, SEQ_LEN)


def to_tokens(values, kinds):
    v = values.reshape(kinds * 128, 8, 128).transpose(1, 0, 2)
    v = lax.all_to_all(v, SEQ, 0, 0, tiled=True)
    v = v.reshape(2, 4, kinds, 128, 128).transpose(2, 1, 3, 0, 4)
    return v.reshape(kinds * 512, 256)


def attend_forward(packed):
    factor = HEAD ** (-0.5)
    scores = jnp.einsum("hcq,hck->hqk", packed[0], packed[1], preferred_element_type=f32) * factor
    highest = jnp.max(scores, axis=-1, keepdims=True)
    exps = jnp.exp(scores - highest)
    total = jnp.sum(exps, axis=-1, keepdims=True)
    low = (exps / total).astype(bf16)
    blended = jnp.einsum("hqk,hck->hcq", low, packed[2], preferred_element_type=f32)
    return blended.astype(bf16).reshape(128, SEQ_LEN), (highest + jnp.log(total))[..., 0]


def attend_backward(packed, logsum, grad):
    factor = HEAD ** (-0.5)
    queries, keys, values = packed[0], packed[1], packed[2]
    scores = jnp.einsum("hcq,hck->hqk", queries, keys, preferred_element_type=f32) * factor
    probs = jnp.exp(scores - logsum[..., None])
    grad_probs = jnp.einsum("hcq,hck->hqk", grad, values, preferred_element_type=f32)
    grad_values = jnp.einsum("hqk,hcq->hck", probs.astype(bf16), grad, preferred_element_type=f32)
    grad_scores = probs * (grad_probs - jnp.sum(probs * grad_probs, axis=-1, keepdims=True))
    grad_scores = grad_scores.astype(bf16)
    grad_queries = jnp.einsum("hqk,hck->hcq", grad_scores, keys, preferred_element_type=f32) * factor
    grad_keys = jnp.einsum("hqk,hcq->hck", grad_scores, queries, preferred_element_type=f32) * factor
    return jnp.stack([grad_queries, grad_keys, grad_values]).astype(bf16)


def on_device(
    tokens,
    w_qkv,
    bias_qv,
    w_out,
    bias_out,
    gain_attn,
    shift_attn,
    w_up,
    bias_up,
    w_down,
    bias_down,
    gain_ffn,
    shift_ffn,
    cotangent,
):
    core = lax.axis_index(CORE)
    traded = trade(
        jnp.concatenate([w_qkv.reshape(LAYERS, 192, 128), w_up.reshape(LAYERS, 256, 128)], axis=1)
    )
    pack = jnp.concatenate(
        [
            traded,
            w_out,
            w_down.reshape(LAYERS, 64, 4, 128).transpose(0, 2, 1, 3).reshape(LAYERS, 256, 128),
        ],
        axis=1,
    )
    every = lax.all_gather(pack, CHIPS, axis=0, tiled=False).reshape(4, 4, 2, 2, LAYERS, 768, 128)
    weights = []
    for l in range(LAYERS):
        e = every[:, :, :, :, l]
        wq = e[..., :192, :].reshape(4, 4, 2, 2, 3, 64, 128)
        wq = wq.transpose(4, 1, 3, 5, 0, 2, 6).reshape(1536, 1024)
        wu = e[..., 192:448, :].transpose(1, 3, 4, 0, 2, 5).reshape(2048, 1024)
        wo = e[..., 448:512, :].transpose(1, 2, 3, 4, 0, 5).reshape(1024, 512)
        wd = e[..., 512:, :].reshape(4, 4, 2, 2, 4, 64, 128)
        wd = wd.transpose(1, 2, 3, 5, 0, 4, 6).reshape(1024, 2048)
        weights.append((wq, wo, wu, wd))

    small = jnp.concatenate(
        [
            v.reshape(-1)
            for v in (bias_qv, bias_out, gain_attn, shift_attn, bias_down, gain_ffn, shift_ffn, bias_up)
        ]
    )
    small = lax.all_to_all(
        jnp.broadcast_to(small[None], (16, small.shape[0])), COL, 0, 0, tiled=True
    )
    b_qv = small[:, :256].reshape(4, 2, 2, LAYERS, 2, 64)
    b_qv = pick(b_qv, core, 1).transpose(2, 3, 0, 1, 4).reshape(LAYERS, 2, 512)
    features = small[:, 256:1024].reshape(16, 6, LAYERS, 64).transpose(1, 2, 0, 3).reshape(6, LAYERS, D)
    b_out, g_attn, s_attn, b_down, g_ffn, s_ffn = features
    b_up = small[:, 1024:].reshape(4, 2, 2, LAYERS, 256)
    b_up = pick(b_up, core, 1).transpose(2, 0, 1, 3).reshape(LAYERS, 2048)

    stream = lax.all_to_all(tokens, COL, 1, 0, tiled=True).astype(f32)
    back = lax.all_to_all(cotangent, COL, 1, 0, tiled=True).astype(f32)
    stored = []
    for l in range(LAYERS):
        wq, wo, wu, wd = weights[l]
        seen = core_gather(stream.astype(bf16))
        bias = jnp.concatenate([b_qv[l, 0], jnp.zeros((512,), f32), b_qv[l, 1]])
        qkv = (dot(wq, seen, 1, 0) + bias[:, None]).astype(bf16)
        packed = to_heads(qkv, 3)
        blended, logsum = attend_forward(packed)
        blended = to_tokens(blended, 1)
        attn_out = core_reduce(dot(wo, blended, 1, 0)) + b_out[l][:, None]
        first, n_attn, i_attn = norm_forward(stream + attn_out, g_attn[l], s_attn[l])
        first_seen = core_gather(first.astype(bf16))
        upper = dot(wu, first_seen, 1, 0) + b_up[l][:, None]
        active = jax.nn.gelu(upper, approximate=False).astype(bf16)
        lower = core_reduce(dot(wd, active, 1, 0)) + b_down[l][:, None]
        stream, n_ffn, i_ffn = norm_forward(first + lower, g_ffn[l], s_ffn[l])
        stored.append(
            (seen, packed, logsum, blended, n_attn, i_attn, first_seen, upper, active, n_ffn, i_ffn)
        )
    result = lax.all_to_all(stream.astype(bf16), COL, 0, 1, tiled=True)

    big = [None] * LAYERS
    minor = [None] * LAYERS
    for l in reversed(range(LAYERS)):
        wq, wo, wu, wd = weights[l]
        (seen, packed, logsum, blended, n_attn, i_attn, first_seen, upper, active, n_ffn, i_ffn) = stored[l]
        grad_sum = norm_backward(back, n_ffn, i_ffn, g_ffn[l])
        p_gain_ffn = jnp.sum(back * n_ffn, axis=1)
        p_shift_ffn = jnp.sum(back, axis=1)
        low = grad_sum.astype(bf16)
        p_down = jnp.sum(low.astype(f32), axis=1)
        low = core_gather(low)
        gw_down = reduce_down(dot(low, active, 1, 1).astype(bf16))
        grad_active = dot(wd, low, 0, 0)
        _, gelu_back = jax.vjp(lambda v: jax.nn.gelu(v, approximate=False), upper)
        grad_upper = gelu_back(grad_active)[0].astype(bf16)
        p_up = jnp.sum(grad_upper.astype(f32), axis=1)
        gw_up = reduce_up(dot(grad_upper, first_seen, 1, 1).astype(bf16))
        grad_first = core_reduce(dot(wu, grad_upper, 0, 0)) + grad_sum
        p_gain_attn = jnp.sum(grad_first * n_attn, axis=1)
        p_shift_attn = jnp.sum(grad_first, axis=1)
        grad_total = norm_backward(grad_first, n_attn, i_attn, g_attn[l])
        low = grad_total.astype(bf16)
        p_out = jnp.sum(low.astype(f32), axis=1)
        low = core_gather(low)
        g_out = dot(low, blended, 1, 1).astype(bf16)
        grad_blended = to_heads(dot(wo, low, 0, 0).astype(bf16), 1)[0]
        grad_qkv = attend_backward(packed, logsum, grad_blended)
        grad_qkv = to_tokens(grad_qkv.reshape(384, SEQ_LEN), 3)
        p_qkv = jnp.sum(grad_qkv.astype(f32).reshape(3, 512, 256), axis=2)
        g_qkv = dot(grad_qkv, seen, 1, 1).astype(bf16)
        gw_qo = reduce_qo(g_qkv, g_out)
        back = core_reduce(dot(wq, grad_qkv, 0, 0)) + grad_total
        swapped = trade(jnp.concatenate([gw_qo[:3].reshape(192, 128), gw_up], axis=0).astype(bf16))
        swapped = swapped.astype(f32)
        big[l] = (swapped[:192].reshape(3, 64, 128), gw_qo[3], swapped[192:], gw_down)
        minor[l] = (p_qkv, p_out, p_gain_attn, p_shift_attn, p_down, p_gain_ffn, p_shift_ffn, p_up)
    grad_tokens = lax.all_to_all(back.astype(bf16), COL, 0, 1, tiled=True).astype(f32)

    mine = (jnp.arange(2) == core).astype(f32)
    qv = jnp.stack([jnp.stack([m[0][0], m[0][2]]) for m in minor])
    qv = qv.reshape(LAYERS, 2, 4, 2, 64).transpose(2, 3, 0, 1, 4)
    qv = (qv[:, None] * mine[None, :, None, None, None, None]).reshape(16, 256)
    up = jnp.stack([m[7] for m in minor]).reshape(LAYERS, 4, 2, 256).transpose(1, 2, 0, 3)
    up = (up[:, None] * mine[None, :, None, None, None]).reshape(16, 512)
    feats = jnp.stack([jnp.stack([m[i] for m in minor]) for i in range(1, 7)])
    feats = feats.reshape(6, LAYERS, 16, 64).transpose(2, 0, 1, 3).reshape(16, 768)
    sums = jnp.concatenate([qv, feats, up], axis=1).reshape(4, 4, 12, 128)
    sums = scatter_axis(lambda i: pick(sums, i, 0), X)
    sums2 = scatter_axis(lambda i: pick(sums, i, 0), Z)
    sums2 = sum_axis(sums2, Y)
    sums2 = sums2 + lax.ppermute(sums2, CORE, [(0, 1), (1, 0)])
    flat = sums2.reshape(1536)
    o_qv = flat[:256].reshape(LAYERS, 2, 64)
    o_out, o_gain_attn, o_shift_attn, o_down, o_gain_ffn, o_shift_ffn = flat[256:1024].reshape(6, LAYERS, 64)
    o_up = flat[1024:].reshape(LAYERS, 256)
    gw_qkv, gw_out, gw_up, gw_down = [jnp.stack([b[i] for b in big]) for i in range(4)]
    return (
        result,
        grad_tokens,
        gw_qkv,
        o_qv,
        gw_out,
        o_out,
        o_gain_attn,
        o_shift_attn,
        gw_up,
        o_up,
        gw_down,
        o_down,
        o_gain_ffn,
        o_shift_ffn,
    )


def solution(mesh):
    fine = Mesh(mesh.devices.reshape(4, 2, 2, 2, 2, 2), ("y", "k", "xh", "xl", "zh", "zl"))
    row = ("y", "k")
    col = COL
    in_specs = (
        P(col, row),
        P(None, None, col, row),
        P(None, None, col),
        P(None, col, row),
        P(None, col),
        P(None, col),
        P(None, col),
        P(None, col, row),
        P(None, col),
        P(None, col, row),
        P(None, col),
        P(None, col),
        P(None, col),
        P(col, row),
    )
    out_specs = (
        P(col, row),
        P(col, row),
        P(None, None, col, row),
        P(None, None, col),
        P(None, col, row),
        P(None, col),
        P(None, col),
        P(None, col),
        P(None, col, row),
        P(None, col),
        P(None, col, row),
        P(None, col),
        P(None, col),
        P(None, col),
    )
    return jax.shard_map(
        on_device, mesh=fine, in_specs=in_specs, out_specs=out_specs, check_vma=False
    )
```

```python
import jax
import jax.numpy as jnp
from jax import lax
from jax.experimental import pallas as pl
from jax.experimental.pallas import tpu as pltpu
from jax.sharding import Mesh, PartitionSpec as P

HEAD = 64
D = 1024
LAYERS = 2
SEQ_LEN = 1024
epsilon = 1e-05

CORE = "k"
Y = ("y",)
X = ("xh", "xl")
Z = ("zh", "zl")
COL = X + Z
CHIPS = Y + COL
SEQ = ("xl", "zh", "zl")
bf16 = jnp.bfloat16
f32 = jnp.float32


NT = ((1,), (1,))
TN = ((0,), (0,))
NN = ((1,), (0,))


def mm(a, b, dims):
    return lax.dot_general(a, b, (dims, ((), ())), preferred_element_type=f32)


def core_gather(values):
    return lax.all_gather(values, CORE, axis=1, tiled=True)


def core_add(pair):
    keep, send = pair
    return keep + lax.ppermute(send, CORE, [(0, 1), (1, 0)]).astype(f32)


def trade(values):
    return lax.ppermute(values, (CORE, "zh"), [(0, 0), (1, 2), (2, 1), (3, 3)])


def pick(values, index, dim):
    return lax.dynamic_index_in_dim(values, index, dim, keepdims=False)


def reduce_stage(g, axes):
    return jnp.sum(lax.all_to_all(g, axes, 0, 0, tiled=True).astype(f32), axis=0)


def reduce_both(g, first, second):
    h = reduce_stage(g, first).astype(bf16)
    return reduce_stage(h.reshape(16, 256, 128), second)


def sum_axis(values, axes):
    total = values
    for shift in (1, 3, 2):
        total += lax.ppermute(values, axes, [(i, (i + shift) % 4) for i in range(4)])
    return total


def call(kernel, grid, ins, outs, scratch=(), flops=0, moved=0):
    return pl.pallas_call(
        kernel,
        grid=grid,
        in_specs=[spec for spec, _ in ins],
        out_specs=[spec for spec, _ in outs],
        out_shape=[shape for _, shape in outs],
        scratch_shapes=list(scratch),
        compiler_params=pltpu.CompilerParams(vmem_limit_bytes=50 * 1024 * 1024),
        cost_estimate=pl.CostEstimate(flops=flops, bytes_accessed=moved, transcendentals=0),
    )(*[value for _, value in ins])


def whole(value):
    rank = value.ndim
    return (pl.BlockSpec(value.shape, lambda g: (0,) * rank), value)


def scalar(value):
    return (pl.BlockSpec(memory_space=pltpu.SMEM), value)


def out_whole(shape, dtype):
    rank = len(shape)
    return (pl.BlockSpec(shape, lambda g: (0,) * rank), jax.ShapeDtypeStruct(shape, dtype))


def split_cores(core_ref, acc, keep_ref, send_ref):
    first = core_ref[0] == 0
    low, high = acc[:, :128], acc[:, 128:]
    keep_ref[...] = jnp.where(first, low, high)
    send_ref[...] = jnp.where(first, high, low).astype(bf16)


PAIR = (out_whole((D, 128), f32), out_whole((D, 128), bf16))


def w_qkv_spec(l):
    return pl.BlockSpec((4, 1, 2, 2, 1, 192, 128), lambda g: (0, g, 0, 0, l, 0, 0))


def w_out_spec(l):
    return pl.BlockSpec((4, 4, 2, 2, 1, 64, 128), lambda g: (0, 0, 0, 0, l, 3, 0))


def w_up_spec(l):
    return pl.BlockSpec((4, 1, 2, 2, 1, 256, 128), lambda g: (0, g, 0, 0, l, 1, 0))


def w_down_spec(l):
    return pl.BlockSpec((1, 4, 2, 2, 1, 256, 128), lambda g: (g, 0, 0, 0, l, 2, 0))


def rows_by_inputs(w_ref, b):
    return jnp.concatenate([w_ref[y, 0, a, b, 0] for y in range(4) for a in range(2)], axis=1)


def down_block(w_ref):
    rows = []
    for x in range(4):
        for a in range(2):
            for b in range(2):
                blk = w_ref[0, x, a, b, 0]
                rows.append(jnp.concatenate([blk[j * 64 : (j + 1) * 64] for j in range(4)], axis=1))
    return jnp.concatenate(rows, axis=0)


def out_block(w_ref):
    rows = []
    for x in range(4):
        for a in range(2):
            for b in range(2):
                rows.append(jnp.concatenate([w_ref[y, x, a, b, 0] for y in range(4)], axis=1))
    return jnp.concatenate(rows, axis=0)


def qkv_kernel(w_ref, x_ref, bias_ref, o_ref):
    x = x_ref[...]
    for b in range(2):
        r = mm(rows_by_inputs(w_ref, b), x, NN)
        for s in range(2):
            v = (r[:, s * 128 : (s + 1) * 128] + bias_ref[0, b]).astype(bf16)
            for j in range(3):
                o_ref[s, 0, j * 128 + b * 64 : j * 128 + b * 64 + 64, :] = v[j * 64 : (j + 1) * 64]


def run_qkv(l, every, seen, bias):
    out = call(
        qkv_kernel,
        (4,),
        [
            (w_qkv_spec(l), every),
            whole(seen),
            (pl.BlockSpec((1, 2, 192, 128), lambda g: (g, 0, 0, 0)), bias),
        ],
        [
            (
                pl.BlockSpec((2, 1, 384, 128), lambda g: (0, g, 0, 0)),
                jax.ShapeDtypeStruct((2, 4, 384, 128), bf16),
            )
        ],
        flops=2 * 1536 * 1024 * 256,
        moved=5 << 20,
    )[0]
    return out.reshape(8, 384, 128)


def join_heads(ref, rows):
    return jnp.concatenate(
        [jnp.concatenate([ref[s * 4 + h] for h in range(4)], axis=0) for s in range(2)], axis=1
    )


def out_kernel(core_ref, w_ref, b_ref, keep_ref, send_ref, blended_ref):
    blended = join_heads(b_ref, 128)
    blended_ref[...] = blended
    split_cores(core_ref, mm(out_block(w_ref), blended, NN), keep_ref, send_ref)


def run_out(l, core, every, arrived):
    keep, send, blended = call(
        out_kernel,
        (1,),
        [scalar(core), (w_out_spec(l), every), whole(arrived)],
        [*PAIR, out_whole((512, 256), bf16)],
        flops=2 * 1024 * 512 * 256,
        moved=2 << 20,
    )
    return (keep, send), blended


def ffn_kernel(core_ref, up_ref, down_ref, x_ref, bias_ref, keep_ref, send_ref, act_ref, slope_ref, acc):
    g = pl.program_id(0)
    x = x_ref[...]
    acts = []
    for b in range(2):
        r = mm(rows_by_inputs(up_ref, b), x, NN)
        bias = bias_ref[0, b]
        r = r + jnp.concatenate([bias, bias], axis=1)
        half = 0.5 * (1.0 + lax.erf(r * (2.0**-0.5)))
        act = (r * half).astype(bf16)
        slope_ref[b * 256 : (b + 1) * 256, :] = half + r * jnp.exp(-0.5 * r * r) * 0.3989422804014327
        act_ref[b * 256 : (b + 1) * 256, :] = act
        acts.append(act)
    part = mm(down_block(down_ref), jnp.concatenate(acts, axis=0), NN)

    @pl.when(g == 0)
    def _():
        acc[...] = part

    @pl.when(g > 0)
    def _():
        acc[...] += part

    @pl.when(g == 3)
    def _():
        split_cores(core_ref, acc[...], keep_ref, send_ref)


def by_step(rows, columns):
    return pl.BlockSpec((rows, columns), lambda g: (g, 0))


def run_ffn(l, core, every, seen, bias):
    keep, send, act, slope = call(
        ffn_kernel,
        (4,),
        [
            scalar(core),
            (w_up_spec(l), every),
            (w_down_spec(l), every),
            whole(seen),
            (pl.BlockSpec((1, 2, 256, 128), lambda g: (g, 0, 0, 0)), bias),
        ],
        [
            *PAIR,
            (by_step(512, 256), jax.ShapeDtypeStruct((2048, 256), bf16)),
            (by_step(512, 256), jax.ShapeDtypeStruct((2048, 256), f32)),
        ],
        [pltpu.VMEM((D, 256), f32)],
        flops=4 * 2048 * 1024 * 256,
        moved=13 << 20,
    )
    return (keep, send), act, slope


def ffn_back_kernel(
    core_ref, up_ref, down_ref, low_ref, act_ref, slope_ref, x_ref, keep_ref, send_ref, gd_ref, gu_ref, bias_ref, acc
):
    g = pl.program_id(0)
    low = low_ref[...]
    grad_active = mm(down_block(down_ref), low, TN)
    wide = grad_active * slope_ref[...]
    gu = wide.astype(bf16)
    bias_ref[...] = jnp.sum(gu.astype(f32), axis=1, keepdims=True)
    gd = mm(low, act_ref[...], NT).astype(bf16)
    for c in range(16):
        for j in range(4):
            gd_ref[0, c, j * 64 : (j + 1) * 64, :] = gd[c * 64 : (c + 1) * 64, j * 128 : (j + 1) * 128]
    x = x_ref[...]
    part = None
    for b in range(2):
        gub = gu[b * 256 : (b + 1) * 256]
        gw = mm(gub, x, NT).astype(bf16)
        for y in range(4):
            for a in range(2):
                i = y * 2 + a
                gu_ref[0, y, a, b] = gw[:, i * 128 : (i + 1) * 128]
        term = mm(rows_by_inputs(up_ref, b), gub, TN)
        part = term if part is None else part + term

    @pl.when(g == 0)
    def _():
        acc[...] = part

    @pl.when(g > 0)
    def _():
        acc[...] += part

    @pl.when(g == 3)
    def _():
        split_cores(core_ref, acc[...], keep_ref, send_ref)


def run_ffn_back(l, core, every, low, act, slope, seen):
    keep, send, gd, gu, bias = call(
        ffn_back_kernel,
        (4,),
        [
            scalar(core),
            (w_up_spec(l), every),
            (w_down_spec(l), every),
            whole(low),
            (by_step(512, 256), act),
            (by_step(512, 256), slope),
            whole(seen),
        ],
        [
            *PAIR,
            (pl.BlockSpec((1, 16, 256, 128), lambda g: (g, 0, 0, 0)), jax.ShapeDtypeStruct((4, 16, 256, 128), bf16)),
            (
                pl.BlockSpec((1, 4, 2, 2, 256, 128), lambda g: (g, 0, 0, 0, 0, 0)),
                jax.ShapeDtypeStruct((4, 4, 2, 2, 256, 128), bf16),
            ),
            (by_step(512, 1), jax.ShapeDtypeStruct((2048, 1), f32)),
        ],
        [pltpu.VMEM((D, 256), f32)],
        flops=8 * 2048 * 1024 * 256,
        moved=22 << 20,
    )
    return (keep, send), gd, gu, bias


def out_back_kernel(w_ref, low_ref, o_ref):
    r = mm(out_block(w_ref), low_ref[...], TN).astype(bf16)
    for s in range(2):
        for h in range(4):
            o_ref[s * 4 + h] = r[h * 128 : (h + 1) * 128, s * 128 : (s + 1) * 128]


def run_out_back(l, every, low):
    return call(
        out_back_kernel,
        (1,),
        [(w_out_spec(l), every), whole(low)],
        [out_whole((8, 128, 128), bf16)],
        flops=2 * 1024 * 512 * 256,
        moved=2 << 20,
    )[0]


def qkv_back_kernel(core_ref, w_ref, gq_ref, x_ref, low_ref, bl_ref, keep_ref, send_ref, g_ref, bias_ref, acc):
    g = pl.program_id(0)
    x = x_ref[...]
    both = jnp.concatenate([gq_ref[0, 0], gq_ref[1, 0]], axis=1)
    part = None
    for b in range(2):
        gq = jnp.concatenate([both[j * 128 + b * 64 : j * 128 + b * 64 + 64] for j in range(3)], axis=0)
        bias_ref[0, b] = jnp.sum(gq.astype(f32), axis=1, keepdims=True)
        gw = mm(gq, x, NT).astype(bf16)
        for y in range(4):
            for a in range(2):
                i = y * 2 + a
                g_ref[a * 2 + b, y, 0, 0:192, :] = gw[:, i * 128 : (i + 1) * 128]
        term = mm(rows_by_inputs(w_ref, b), gq, TN)
        part = term if part is None else part + term
    go = mm(low_ref[...], bl_ref[...], NT).astype(bf16)
    for z in range(4):
        for y in range(4):
            g_ref[z, y, 0, 192:256, :] = go[z * 64 : (z + 1) * 64, y * 128 : (y + 1) * 128]

    @pl.when(g == 0)
    def _():
        acc[...] = part

    @pl.when(g > 0)
    def _():
        acc[...] += part

    @pl.when(g == 3)
    def _():
        split_cores(core_ref, acc[...], keep_ref, send_ref)


def run_qkv_back(l, core, every, arrived, seen, low, blended):
    keep, send, gqo, bias = call(
        qkv_back_kernel,
        (4,),
        [
            scalar(core),
            (w_qkv_spec(l), every),
            (pl.BlockSpec((2, 1, 384, 128), lambda g: (0, g, 0, 0)), arrived.reshape(2, 4, 384, 128)),
            whole(seen),
            (by_step(256, 256), low),
            whole(blended),
        ],
        [
            *PAIR,
            (
                pl.BlockSpec((4, 4, 1, 256, 128), lambda g: (0, 0, g, 0, 0)),
                jax.ShapeDtypeStruct((4, 4, 4, 256, 128), bf16),
            ),
            (pl.BlockSpec((1, 2, 192, 1), lambda g: (g, 0, 0, 0)), jax.ShapeDtypeStruct((4, 2, 192, 1), f32)),
        ],
        [pltpu.VMEM((D, 256), f32)],
        flops=6 * 2048 * 1024 * 256,
        moved=12 << 20,
    )
    return (keep, send), gqo, bias


FACTOR = HEAD ** (-0.5)
STEP = 256


def join_tokens(ref, top):
    return jnp.concatenate([ref[c, top : top + HEAD] for c in range(8)], axis=1)


def attend_kernel(p_ref, o_ref, log_ref):
    for h in range(2):
        q = join_tokens(p_ref, h * 64)
        k = join_tokens(p_ref, 128 + h * 64)
        v = join_tokens(p_ref, 256 + h * 64)
        for c in range(SEQ_LEN // STEP):
            scores = mm(k, q[:, c * STEP : (c + 1) * STEP], TN) * FACTOR
            highest = jnp.max(scores, axis=0, keepdims=True)
            exps = jnp.exp(scores - highest)
            total = jnp.sum(exps, axis=0, keepdims=True)
            low = (exps * (1.0 / total)).astype(bf16)
            out = mm(v, low, NN).astype(bf16)
            log_ref[h : h + 1, c * STEP : (c + 1) * STEP] = highest + jnp.log(total)
            for n in range(STEP // 128):
                o_ref[c * (STEP // 128) + n, h * 64 : h * 64 + 64, :] = out[:, n * 128 : (n + 1) * 128]


def run_attend(packed):
    return call(
        attend_kernel,
        (1,),
        [whole(packed)],
        [out_whole((8, 128, 128), bf16), out_whole((2, SEQ_LEN), f32)],
        flops=8 * 1024 * 1024 * 128,
        moved=1 << 20,
    )


def attend_back_kernel(p_ref, b_ref, log_ref, o_ref):
    for h in range(2):
        q = join_tokens(p_ref, h * 64)
        k = join_tokens(p_ref, 128 + h * 64)
        v = join_tokens(p_ref, 256 + h * 64)
        gb = join_tokens(b_ref, h * 64)
        gk = gv = None
        for c in range(SEQ_LEN // STEP):
            cols = slice(c * STEP, (c + 1) * STEP)
            qc, gc = q[:, cols], gb[:, cols]
            probs = jnp.exp(mm(k, qc, TN) * FACTOR - log_ref[h : h + 1, cols])
            gp = mm(v, gc, TN)
            row = jnp.sum(probs * gp, axis=0, keepdims=True)
            ds = (probs * (gp - row)).astype(bf16)
            tv = mm(gc, probs.astype(bf16), NT)
            tk = mm(qc, ds, NT)
            gv = tv if gv is None else gv + tv
            gk = tk if gk is None else gk + tk
            gq = (mm(k, ds, NN) * FACTOR).astype(bf16)
            for n in range(STEP // 128):
                o_ref[c * (STEP // 128) + n, h * 64 : h * 64 + 64, :] = gq[:, n * 128 : (n + 1) * 128]
        gk = (gk * FACTOR).astype(bf16)
        gv = gv.astype(bf16)
        for c in range(8):
            o_ref[c, 128 + h * 64 : 192 + h * 64, :] = gk[:, c * 128 : (c + 1) * 128]
            o_ref[c, 256 + h * 64 : 320 + h * 64, :] = gv[:, c * 128 : (c + 1) * 128]


def run_attend_back(packed, grad, log):
    return call(
        attend_back_kernel,
        (1,),
        [whole(packed), whole(grad), whole(log)],
        [out_whole((8, 384, 128), bf16)],
        flops=20 * 1024 * 1024 * 128,
        moved=2 << 20,
    )[0]


def seq_swap(values):
    return lax.all_to_all(values, SEQ, 0, 0, tiled=True)


def norm_forward(summed, gain, shift):
    centre = jnp.mean(summed, axis=0, keepdims=True)
    centred = summed - centre
    variance = jnp.mean(centred * centred, axis=0, keepdims=True)
    scaled = lax.rsqrt(variance + epsilon)
    normed = centred * scaled
    return normed * gain[:, None] + shift[:, None], normed, scaled


def norm_backward(incoming, normed, scaled, gain):
    grad_norm = incoming * gain[:, None]
    plain = jnp.mean(grad_norm, axis=0, keepdims=True)
    cross = jnp.mean(grad_norm * normed, axis=0, keepdims=True)
    return scaled * (grad_norm - plain - normed * cross)


def on_device(
    tokens,
    w_qkv,
    bias_qv,
    w_out,
    bias_out,
    gain_attn,
    shift_attn,
    w_up,
    bias_up,
    w_down,
    bias_down,
    gain_ffn,
    shift_ffn,
    cotangent,
):
    core = lax.axis_index(CORE)
    here = core.astype(jnp.int32).reshape(1)
    traded = trade(
        jnp.concatenate([w_qkv.reshape(LAYERS, 192, 128), w_up.reshape(LAYERS, 256, 128)], axis=1)
    )
    pack = jnp.concatenate(
        [
            traded[:, :192],
            w_out,
            traded[:, 192:],
            w_down.reshape(LAYERS, 64, 4, 128).transpose(0, 2, 1, 3).reshape(LAYERS, 256, 128),
        ],
        axis=1,
    )
    every = lax.all_gather(pack, CHIPS, axis=0, tiled=False).reshape(4, 4, 2, 2, LAYERS, 768, 128)

    small = jnp.concatenate(
        [
            v.reshape(-1)
            for v in (bias_qv, bias_out, gain_attn, shift_attn, bias_down, gain_ffn, shift_ffn, bias_up)
        ]
    )
    small = lax.all_to_all(
        jnp.broadcast_to(small[None], (16, small.shape[0])), COL, 0, 0, tiled=True
    )
    b_qv = small[:, :256].reshape(4, 2, 2, LAYERS, 2, 64)
    b_qv = pick(b_qv, core, 1).transpose(2, 0, 1, 3, 4)
    b_qkv = jnp.stack([b_qv[:, :, :, 0], jnp.zeros_like(b_qv[:, :, :, 0]), b_qv[:, :, :, 1]], axis=3)
    b_qkv = jnp.broadcast_to(b_qkv.reshape(LAYERS, 4, 2, 192, 1), (LAYERS, 4, 2, 192, 128))
    features = small[:, 256:1024].reshape(16, 6, LAYERS, 64).transpose(1, 2, 0, 3).reshape(6, LAYERS, D)
    b_out, g_attn, s_attn, b_down, g_ffn, s_ffn = features
    b_up = small[:, 1024:].reshape(4, 2, 2, LAYERS, 256)
    b_up = pick(b_up, core, 1).transpose(2, 0, 1, 3)
    b_up = jnp.broadcast_to(b_up[..., None], (LAYERS, 4, 2, 256, 128))

    stream = lax.all_to_all(tokens, COL, 1, 0, tiled=True).astype(f32)
    back = lax.all_to_all(cotangent, COL, 1, 0, tiled=True).astype(f32)
    stored = []
    for l in range(LAYERS):
        seen = core_gather(stream.astype(bf16))
        packed = seq_swap(run_qkv(l, every, seen, b_qkv[l]))
        mixed, log = run_attend(packed)
        pair, blended = run_out(l, here, every, seq_swap(mixed))
        attn_out = core_add(pair) + b_out[l][:, None]
        first, n_attn, i_attn = norm_forward(stream + attn_out, g_attn[l], s_attn[l])
        first_seen = core_gather(first.astype(bf16))
        pair, active, slope = run_ffn(l, here, every, first_seen, b_up[l])
        lower = core_add(pair) + b_down[l][:, None]
        stream, n_ffn, i_ffn = norm_forward(first + lower, g_ffn[l], s_ffn[l])
        stored.append((seen, packed, log, blended, n_attn, i_attn, first_seen, active, slope, n_ffn, i_ffn))
    result = lax.all_to_all(stream.astype(bf16), COL, 0, 1, tiled=True)

    big = [None] * LAYERS
    minor = [None] * LAYERS
    for l in reversed(range(LAYERS)):
        (seen, packed, log, blended, n_attn, i_attn, first_seen, active, slope, n_ffn, i_ffn) = stored[l]
        grad_sum = norm_backward(back, n_ffn, i_ffn, g_ffn[l])
        p_gain_ffn = jnp.sum(back * n_ffn, axis=1)
        p_shift_ffn = jnp.sum(back, axis=1)
        low = grad_sum.astype(bf16)
        p_down = jnp.sum(low.astype(f32), axis=1)
        pair, gd, gu, p_up = run_ffn_back(l, here, every, core_gather(low), active, slope, first_seen)
        gw_down = reduce_both(gd, Y, COL)
        gw_up = reduce_both(gu.reshape(4, 16, 256, 128), X, ("y",) + Z)
        grad_first = core_add(pair) + grad_sum
        p_gain_attn = jnp.sum(grad_first * n_attn, axis=1)
        p_shift_attn = jnp.sum(grad_first, axis=1)
        grad_total = norm_backward(grad_first, n_attn, i_attn, g_attn[l])
        low = grad_total.astype(bf16)
        p_out = jnp.sum(low.astype(f32), axis=1)
        low = core_gather(low)
        grad_blended = seq_swap(run_out_back(l, every, low))
        grad_qkv = seq_swap(run_attend_back(packed, grad_blended, log))
        pair, gqo, p_qkv = run_qkv_back(l, here, every, grad_qkv, seen, low, blended)
        gw_qo = reduce_both(gqo.reshape(4, 16, 256, 128), Z, ("y",) + X)
        back = core_add(pair) + grad_total
        swapped = trade(jnp.concatenate([gw_qo[:192], gw_up], axis=0).astype(bf16)).astype(f32)
        gw_down = gw_down.reshape(4, 64, 128).transpose(1, 0, 2).reshape(64, 512)
        big[l] = (swapped[:192].reshape(3, 64, 128), gw_qo[192:], swapped[192:], gw_down)
        minor[l] = (p_qkv, p_out, p_gain_attn, p_shift_attn, p_down, p_gain_ffn, p_shift_ffn, p_up)
    grad_tokens = lax.all_to_all(back.astype(bf16), COL, 0, 1, tiled=True).astype(f32)

    mine = (jnp.arange(2) == core).astype(f32)
    qv = jnp.stack([m[0].reshape(4, 2, 3, 64)[:, :, ::2] for m in minor])
    qv = qv.transpose(1, 2, 0, 3, 4)
    qv = (qv[:, None] * mine[None, :, None, None, None, None]).reshape(16, 256)
    up = jnp.stack([m[7] for m in minor]).reshape(LAYERS, 4, 2, 256).transpose(1, 2, 0, 3)
    up = (up[:, None] * mine[None, :, None, None, None]).reshape(16, 512)
    feats = jnp.stack([jnp.stack([m[i] for m in minor]) for i in range(1, 7)])
    feats = feats.reshape(6, LAYERS, 16, 64).transpose(2, 0, 1, 3).reshape(16, 768)
    sums = jnp.concatenate([qv, feats, up], axis=1).reshape(4, 4, 12, 128)
    sums2 = sum_axis(reduce_stage(sums.reshape(16, 12, 128), COL), Y)
    sums2 = sums2 + lax.ppermute(sums2, CORE, [(0, 1), (1, 0)])
    flat = sums2.reshape(1536)
    o_qv = flat[:256].reshape(LAYERS, 2, 64)
    o_out, o_gain_attn, o_shift_attn, o_down, o_gain_ffn, o_shift_ffn = flat[256:1024].reshape(6, LAYERS, 64)
    o_up = flat[1024:].reshape(LAYERS, 256)
    gw_qkv, gw_out, gw_up, gw_down = [jnp.stack([b[i] for b in big]) for i in range(4)]
    return (
        result,
        grad_tokens,
        gw_qkv,
        o_qv,
        gw_out,
        o_out,
        o_gain_attn,
        o_shift_attn,
        gw_up,
        o_up,
        gw_down,
        o_down,
        o_gain_ffn,
        o_shift_ffn,
    )


def solution(mesh):
    fine = Mesh(mesh.devices.reshape(4, 2, 2, 2, 2, 2), ("y", "k", "xh", "xl", "zh", "zl"))
    row = ("y", "k")
    col = COL
    in_specs = (
        P(col, row),
        P(None, None, col, row),
        P(None, None, col),
        P(None, col, row),
        P(None, col),
        P(None, col),
        P(None, col),
        P(None, col, row),
        P(None, col),
        P(None, col, row),
        P(None, col),
        P(None, col),
        P(None, col),
        P(col, row),
    )
    out_specs = (
        P(col, row),
        P(col, row),
        P(None, None, col, row),
        P(None, None, col),
        P(None, col, row),
        P(None, col),
        P(None, col),
        P(None, col),
        P(None, col, row),
        P(None, col),
        P(None, col, row),
        P(None, col),
        P(None, col),
        P(None, col),
    )
    return jax.shard_map(
        on_device, mesh=fine, in_specs=in_specs, out_specs=out_specs, check_vma=False
    )
```

```python
from functools import partial
from typing import NamedTuple

import jax
import jax.numpy as jnp
from jax import lax
from jax.experimental import pallas as pl
from jax.experimental.pallas import tpu as pltpu
from jax.sharding import Mesh, PartitionSpec as P

HEAD = 64
D = 1024
LAYERS = 2
SEQ_LEN = 1024
epsilon = 1e-05

CORE = "k"
Y = ("y",)
X = ("xh", "xl")
Z = ("zh", "zl")
COL = X + Z
CHIPS = Y + COL
SEQ = ("xl", "zh", "zl")
bf16 = jnp.bfloat16
f32 = jnp.float32


NT = ((1,), (1,))
TN = ((0,), (0,))
NN = ((1,), (0,))


def mm(a, b, dims):
    return lax.dot_general(a, b, (dims, ((), ())), preferred_element_type=f32)


def core_gather(values):
    return lax.all_gather(values, CORE, axis=1, tiled=True)


def core_add(pair):
    keep, send = pair
    return keep + lax.ppermute(send, CORE, [(0, 1), (1, 0)]).astype(f32)


def trade(values):
    return lax.ppermute(values, (CORE, "zh"), [(0, 0), (1, 2), (2, 1), (3, 3)])


def pick(values, index, dim):
    return lax.dynamic_index_in_dim(values, index, dim, keepdims=False)


def reduce_stage(g, axes):
    return jnp.sum(lax.all_to_all(g, axes, 0, 0, tiled=True).astype(f32), axis=0)


def after(values, *others):
    return lax.optimization_barrier((values, *others))[0]


class Weights(NamedTuple):
    qo: jax.Array
    up: jax.Array
    down: jax.Array
    up_at: int
    down_at: int


def sum_axis(values, axes):
    total = values
    for shift in (1, 3, 2):
        total += lax.ppermute(values, axes, [(i, (i + shift) % 4) for i in range(4)])
    return total


def call(kernel, grid, ins, outs, scratch=(), flops=0, moved=0):
    return pl.pallas_call(
        kernel,
        grid=grid,
        in_specs=[spec for spec, _ in ins],
        out_specs=[spec for spec, _ in outs],
        out_shape=[shape for _, shape in outs],
        scratch_shapes=list(scratch),
        compiler_params=pltpu.CompilerParams(vmem_limit_bytes=50 * 1024 * 1024),
        cost_estimate=pl.CostEstimate(flops=flops, bytes_accessed=moved, transcendentals=0),
    )(*[value for _, value in ins])


def whole(value):
    rank = value.ndim
    return (pl.BlockSpec(value.shape, lambda g: (0,) * rank), value)


def scalar(value):
    return (pl.BlockSpec(memory_space=pltpu.SMEM), value)


def out_whole(shape, dtype):
    rank = len(shape)
    return (pl.BlockSpec(shape, lambda g: (0,) * rank), jax.ShapeDtypeStruct(shape, dtype))


def split_cores(core_ref, acc, keep_ref, send_ref):
    first = core_ref[0] == 0
    low, high = acc[:, :128], acc[:, 128:]
    keep_ref[...] = jnp.where(first, low, high)
    send_ref[...] = jnp.where(first, high, low).astype(bf16)


PAIR = (out_whole((D, 128), f32), out_whole((D, 128), bf16))


def w_qkv_spec():
    return pl.BlockSpec((4, 1, 2, 2, 192, 128), lambda g: (0, g, 0, 0, 0, 0))


def w_out_spec():
    return pl.BlockSpec((4, 4, 2, 2, 64, 128), lambda g: (0, 0, 0, 0, 3, 0))


def w_up_spec(i):
    return pl.BlockSpec((4, 1, 2, 2, 256, 128), lambda g: (0, g, 0, 0, i, 0))


def w_down_spec(i):
    return pl.BlockSpec((1, 4, 2, 2, 256, 128), lambda g: (g, 0, 0, 0, i, 0))


def rows_by_inputs(w_ref, b):
    return jnp.concatenate([w_ref[y, 0, a, b] for y in range(4) for a in range(2)], axis=1)


def down_block(w_ref):
    rows = []
    for x in range(4):
        for a in range(2):
            for b in range(2):
                blk = w_ref[0, x, a, b]
                rows.append(jnp.concatenate([blk[j * 64 : (j + 1) * 64] for j in range(4)], axis=1))
    return jnp.concatenate(rows, axis=0)


def out_block(w_ref):
    rows = []
    for x in range(4):
        for a in range(2):
            for b in range(2):
                rows.append(jnp.concatenate([w_ref[y, x, a, b] for y in range(4)], axis=1))
    return jnp.concatenate(rows, axis=0)


def qkv_kernel(w_ref, x_ref, bias_ref, o_ref):
    x = x_ref[...]
    for b in range(2):
        r = mm(rows_by_inputs(w_ref, b), x, NN)
        for s in range(2):
            v = (r[:, s * 128 : (s + 1) * 128] + bias_ref[0, b]).astype(bf16)
            for j in range(3):
                o_ref[s, 0, j * 128 + b * 64 : j * 128 + b * 64 + 64, :] = v[j * 64 : (j + 1) * 64]


def run_qkv(w, seen, bias):
    out = call(
        qkv_kernel,
        (4,),
        [
            (w_qkv_spec(), w.qo),
            whole(seen),
            (pl.BlockSpec((1, 2, 192, 128), lambda g: (g, 0, 0, 0)), bias),
        ],
        [
            (
                pl.BlockSpec((2, 1, 384, 128), lambda g: (0, g, 0, 0)),
                jax.ShapeDtypeStruct((2, 4, 384, 128), bf16),
            )
        ],
        flops=2 * 1536 * 1024 * 256,
        moved=5 << 20,
    )[0]
    return out.reshape(8, 384, 128)


def join_heads(ref, rows):
    return jnp.concatenate(
        [jnp.concatenate([ref[s * 4 + h] for h in range(4)], axis=0) for s in range(2)], axis=1
    )


def out_kernel(core_ref, w_ref, b_ref, keep_ref, send_ref, blended_ref):
    blended = join_heads(b_ref, 128)
    blended_ref[...] = blended
    split_cores(core_ref, mm(out_block(w_ref), blended, NN), keep_ref, send_ref)


def run_out(w, core, arrived):
    keep, send, blended = call(
        out_kernel,
        (1,),
        [scalar(core), (w_out_spec(), w.qo), whole(arrived)],
        [*PAIR, out_whole((512, 256), bf16)],
        flops=2 * 1024 * 512 * 256,
        moved=2 << 20,
    )
    return (keep, send), blended


def ffn_kernel(core_ref, up_ref, down_ref, x_ref, bias_ref, keep_ref, send_ref, act_ref, slope_ref, acc):
    g = pl.program_id(0)
    x = x_ref[...]
    acts = []
    for b in range(2):
        r = mm(rows_by_inputs(up_ref, b), x, NN)
        bias = bias_ref[0, b]
        r = r + jnp.concatenate([bias, bias], axis=1)
        half = 0.5 * (1.0 + lax.erf(r * (2.0**-0.5)))
        act = (r * half).astype(bf16)
        slope_ref[b * 256 : (b + 1) * 256, :] = half + r * jnp.exp(-0.5 * r * r) * 0.3989422804014327
        act_ref[b * 256 : (b + 1) * 256, :] = act
        acts.append(act)
    part = mm(down_block(down_ref), jnp.concatenate(acts, axis=0), NN)

    @pl.when(g == 0)
    def _():
        acc[...] = part

    @pl.when(g > 0)
    def _():
        acc[...] += part

    @pl.when(g == 3)
    def _():
        split_cores(core_ref, acc[...], keep_ref, send_ref)


def by_step(rows, columns):
    return pl.BlockSpec((rows, columns), lambda g: (g, 0))


def run_ffn(w, core, seen, bias):
    keep, send, act, slope = call(
        ffn_kernel,
        (4,),
        [
            scalar(core),
            (w_up_spec(w.up_at), w.up),
            (w_down_spec(w.down_at), w.down),
            whole(seen),
            (pl.BlockSpec((1, 2, 256, 128), lambda g: (g, 0, 0, 0)), bias),
        ],
        [
            *PAIR,
            (by_step(512, 256), jax.ShapeDtypeStruct((2048, 256), bf16)),
            (by_step(512, 256), jax.ShapeDtypeStruct((2048, 256), f32)),
        ],
        [pltpu.VMEM((D, 256), f32)],
        flops=4 * 2048 * 1024 * 256,
        moved=13 << 20,
    )
    return (keep, send), act, slope


def ffn_back_kernel(core_ref, up_ref, down_ref, low_ref, slope_ref, keep_ref, send_ref, bias_ref, g_ref, acc):
    g = pl.program_id(0)
    low = low_ref[...]
    gu = (mm(down_block(down_ref), low, TN) * slope_ref[...]).astype(bf16)
    bias_ref[...] = jnp.sum(gu.astype(f32), axis=1, keepdims=True)
    g_ref[0, 0:256] = low_ref[pl.ds(pl.multiple_of(g * 256, 256), 256), :]
    g_ref[0, 256:768] = gu
    up = jnp.concatenate([rows_by_inputs(up_ref, b) for b in range(2)], axis=0)
    part = mm(up, gu, TN)

    @pl.when(g == 0)
    def _():
        acc[...] = part

    @pl.when(g > 0)
    def _():
        acc[...] += part

    @pl.when(g == 3)
    def _():
        split_cores(core_ref, acc[...], keep_ref, send_ref)


def run_ffn_back(w, core, low, slope):
    keep, send, bias, grads = call(
        ffn_back_kernel,
        (4,),
        [
            scalar(core),
            (w_up_spec(w.up_at), w.up),
            (w_down_spec(w.down_at), w.down),
            whole(low),
            (by_step(512, 256), slope),
        ],
        [
            *PAIR,
            (by_step(512, 1), jax.ShapeDtypeStruct((2048, 1), f32)),
            (pl.BlockSpec((1, 768, 256), lambda g: (g, 0, 0)), jax.ShapeDtypeStruct((4, 768, 256), bf16)),
        ],
        [pltpu.VMEM((D, 256), f32)],
        flops=4 * 2048 * 1024 * 256,
        moved=14 << 20,
    )
    return (keep, send), grads, bias


def wide(ref, top, rows):
    return jnp.concatenate([ref[i, top : top + rows] for i in range(4)], axis=1)


def ffn_grad_kernel(g_ref, act_ref, seen_ref, o_ref):
    gd = mm(wide(g_ref, 0, 256), wide(act_ref, 0, 512), NT).astype(bf16)
    gu = mm(wide(g_ref, 256, 512), wide(seen_ref, 0, 256), NT).astype(bf16)
    for a in range(2):
        for b in range(2):
            z = a * 2 + b
            o_ref[0, z, 0:256, :] = gu[b * 256 : (b + 1) * 256, a * 128 : (a + 1) * 128]
            for j in range(4):
                o_ref[0, z, 256 + j * 64 : 320 + j * 64, :] = gd[z * 64 : (z + 1) * 64, j * 128 : (j + 1) * 128]


def inputs_spec(rows, base):
    return pl.BlockSpec((4, rows, 256), lambda g: (0, base + g, 0))


def run_ffn_grad(arrived, inputs):
    return call(
        ffn_grad_kernel,
        (4,),
        [whole(arrived), (inputs_spec(512, 0), inputs), (inputs_spec(256, 8), inputs)],
        [(pl.BlockSpec((1, 4, 512, 128), lambda g: (g, 0, 0, 0)), jax.ShapeDtypeStruct((4, 4, 512, 128), bf16))],
        flops=4 * 2048 * 1024 * 256,
        moved=14 << 20,
    )[0]


def attend_grad_kernel(g_ref, bl_ref, seen_ref, o_ref):
    go = mm(wide(g_ref, 0, 256), wide(bl_ref, 0, 128), NT).astype(bf16)
    gq = mm(wide(g_ref, 256, 384), wide(seen_ref, 0, 256), NT).astype(bf16)
    for a in range(2):
        for b in range(2):
            z = a * 2 + b
            for j in range(3):
                top = j * 128 + b * 64
                o_ref[0, z, j * 64 : (j + 1) * 64, :] = gq[top : top + 64, a * 128 : (a + 1) * 128]
            o_ref[0, z, 192:256, :] = go[z * 64 : (z + 1) * 64]


def run_attend_grad(arrived, inputs):
    return call(
        attend_grad_kernel,
        (4,),
        [whole(arrived), (inputs_spec(128, 24), inputs), (inputs_spec(256, 14), inputs)],
        [(pl.BlockSpec((1, 4, 256, 128), lambda g: (g, 0, 0, 0)), jax.ShapeDtypeStruct((4, 4, 256, 128), bf16))],
        flops=2 * 2048 * 1024 * 256,
        moved=7 << 20,
    )[0]


def out_back_kernel(w_ref, low_ref, o_ref):
    r = mm(out_block(w_ref), low_ref[...], TN).astype(bf16)
    for s in range(2):
        for h in range(4):
            o_ref[s * 4 + h] = r[h * 128 : (h + 1) * 128, s * 128 : (s + 1) * 128]


def run_out_back(w, low):
    return call(
        out_back_kernel,
        (1,),
        [(w_out_spec(), w.qo), whole(low)],
        [out_whole((8, 128, 128), bf16)],
        flops=2 * 1024 * 512 * 256,
        moved=2 << 20,
    )[0]


def qkv_back_kernel(core_ref, w_ref, gq_ref, low_ref, keep_ref, send_ref, g_ref, bias_ref, acc):
    g = pl.program_id(0)
    both = jnp.concatenate([gq_ref[0, 0], gq_ref[1, 0]], axis=1)
    g_ref[0, 0:256] = low_ref[...]
    g_ref[0, 256:640] = both
    part = None
    for b in range(2):
        gq = jnp.concatenate([both[j * 128 + b * 64 : j * 128 + b * 64 + 64] for j in range(3)], axis=0)
        bias_ref[0, b] = jnp.sum(gq.astype(f32), axis=1, keepdims=True)
        term = mm(rows_by_inputs(w_ref, b), gq, TN)
        part = term if part is None else part + term

    @pl.when(g == 0)
    def _():
        acc[...] = part

    @pl.when(g > 0)
    def _():
        acc[...] += part

    @pl.when(g == 3)
    def _():
        split_cores(core_ref, acc[...], keep_ref, send_ref)


def run_qkv_back(w, core, arrived, low):
    keep, send, grads, bias = call(
        qkv_back_kernel,
        (4,),
        [
            scalar(core),
            (w_qkv_spec(), w.qo),
            (pl.BlockSpec((2, 1, 384, 128), lambda g: (0, g, 0, 0)), arrived.reshape(2, 4, 384, 128)),
            (by_step(256, 256), low),
        ],
        [
            *PAIR,
            (pl.BlockSpec((1, 640, 256), lambda g: (g, 0, 0)), jax.ShapeDtypeStruct((4, 640, 256), bf16)),
            (pl.BlockSpec((1, 2, 192, 1), lambda g: (g, 0, 0, 0)), jax.ShapeDtypeStruct((4, 2, 192, 1), f32)),
        ],
        [pltpu.VMEM((D, 256), f32)],
        flops=2 * 1536 * 1024 * 256,
        moved=7 << 20,
    )
    return (keep, send), grads, bias


FACTOR = HEAD ** (-0.5)
STEP = 256


def join_tokens(ref, top):
    return jnp.concatenate([ref[c, top : top + HEAD] for c in range(8)], axis=1)


def attend_kernel(p_ref, o_ref, log_ref):
    for h in range(2):
        q = join_tokens(p_ref, h * 64)
        k = join_tokens(p_ref, 128 + h * 64)
        v = join_tokens(p_ref, 256 + h * 64)
        for c in range(SEQ_LEN // STEP):
            scores = mm(k, q[:, c * STEP : (c + 1) * STEP], TN) * FACTOR
            highest = jnp.max(scores, axis=0, keepdims=True)
            exps = jnp.exp(scores - highest)
            total = jnp.sum(exps, axis=0, keepdims=True)
            low = (exps * (1.0 / total)).astype(bf16)
            out = mm(v, low, NN).astype(bf16)
            log_ref[h : h + 1, c * STEP : (c + 1) * STEP] = highest + jnp.log(total)
            for n in range(STEP // 128):
                o_ref[c * (STEP // 128) + n, h * 64 : h * 64 + 64, :] = out[:, n * 128 : (n + 1) * 128]


def run_attend(packed):
    return call(
        attend_kernel,
        (1,),
        [whole(packed)],
        [out_whole((8, 128, 128), bf16), out_whole((2, SEQ_LEN), f32)],
        flops=8 * 1024 * 1024 * 128,
        moved=1 << 20,
    )


def attend_back_kernel(p_ref, b_ref, log_ref, o_ref):
    for h in range(2):
        q = join_tokens(p_ref, h * 64)
        k = join_tokens(p_ref, 128 + h * 64)
        v = join_tokens(p_ref, 256 + h * 64)
        gb = join_tokens(b_ref, h * 64)
        gk = gv = None
        for c in range(SEQ_LEN // STEP):
            cols = slice(c * STEP, (c + 1) * STEP)
            qc, gc = q[:, cols], gb[:, cols]
            probs = jnp.exp(mm(k, qc, TN) * FACTOR - log_ref[h : h + 1, cols])
            gp = mm(v, gc, TN)
            row = jnp.sum(probs * gp, axis=0, keepdims=True)
            ds = (probs * (gp - row)).astype(bf16)
            tv = mm(gc, probs.astype(bf16), NT)
            tk = mm(qc, ds, NT)
            gv = tv if gv is None else gv + tv
            gk = tk if gk is None else gk + tk
            gq = (mm(k, ds, NN) * FACTOR).astype(bf16)
            for n in range(STEP // 128):
                o_ref[c * (STEP // 128) + n, h * 64 : h * 64 + 64, :] = gq[:, n * 128 : (n + 1) * 128]
        gk = (gk * FACTOR).astype(bf16)
        gv = gv.astype(bf16)
        for c in range(8):
            o_ref[c, 128 + h * 64 : 192 + h * 64, :] = gk[:, c * 128 : (c + 1) * 128]
            o_ref[c, 256 + h * 64 : 320 + h * 64, :] = gv[:, c * 128 : (c + 1) * 128]


def run_attend_back(packed, grad, log):
    return call(
        attend_back_kernel,
        (1,),
        [whole(packed), whole(grad), whole(log)],
        [out_whole((8, 384, 128), bf16)],
        flops=20 * 1024 * 1024 * 128,
        moved=2 << 20,
    )[0]


def seq_swap(values):
    return lax.all_to_all(values, SEQ, 0, 0, tiled=True)


def norm_forward(summed, gain, shift):
    centre = jnp.mean(summed, axis=0, keepdims=True)
    centred = summed - centre
    variance = jnp.mean(centred * centred, axis=0, keepdims=True)
    scaled = lax.rsqrt(variance + epsilon)
    normed = centred * scaled
    return normed * gain[:, None] + shift[:, None], normed, scaled


def norm_backward(incoming, normed, scaled, gain):
    grad_norm = incoming * gain[:, None]
    plain = jnp.mean(grad_norm, axis=0, keepdims=True)
    cross = jnp.mean(grad_norm * normed, axis=0, keepdims=True)
    return scaled * (grad_norm - plain - normed * cross)


def on_device(
    tokens,
    w_qkv,
    bias_qv,
    w_out,
    bias_out,
    gain_attn,
    shift_attn,
    w_up,
    bias_up,
    w_down,
    bias_down,
    gain_ffn,
    shift_ffn,
    cotangent,
):
    core = lax.axis_index(CORE)
    here = core.astype(jnp.int32).reshape(1)
    traded = trade(
        jnp.concatenate([w_qkv.reshape(LAYERS, 192, 128), w_up.reshape(LAYERS, 256, 128)], axis=1)
    )
    pack = jnp.concatenate(
        [
            traded[:, :192],
            w_out,
            traded[:, 192:],
            w_down.reshape(LAYERS, 64, 4, 128).transpose(0, 2, 1, 3).reshape(LAYERS, 256, 128),
        ],
        axis=1,
    )
    weights = []
    for l in range(LAYERS):
        every = lax.all_gather(pack[l], CHIPS, axis=0, tiled=False).reshape(4, 4, 2, 2, 768, 128)
        weights.append(Weights(every, every, every, 1, 2))

    small = jnp.concatenate(
        [
            v.reshape(-1)
            for v in (bias_qv, bias_out, gain_attn, shift_attn, bias_down, gain_ffn, shift_ffn, bias_up)
        ]
    )
    small = lax.all_to_all(
        jnp.broadcast_to(small[None], (16, small.shape[0])), COL, 0, 0, tiled=True
    )
    b_qv = small[:, :256].reshape(4, 2, 2, LAYERS, 2, 64)
    b_qv = pick(b_qv, core, 1).transpose(2, 0, 1, 3, 4)
    b_qkv = jnp.stack([b_qv[:, :, :, 0], jnp.zeros_like(b_qv[:, :, :, 0]), b_qv[:, :, :, 1]], axis=3)
    b_qkv = jnp.broadcast_to(b_qkv.reshape(LAYERS, 4, 2, 192, 1), (LAYERS, 4, 2, 192, 128))
    features = small[:, 256:1024].reshape(16, 6, LAYERS, 64).transpose(1, 2, 0, 3).reshape(6, LAYERS, D)
    b_out, g_attn, s_attn, b_down, g_ffn, s_ffn = features
    b_up = small[:, 1024:].reshape(4, 2, 2, LAYERS, 256)
    b_up = pick(b_up, core, 1).transpose(2, 0, 1, 3)
    b_up = jnp.broadcast_to(b_up[..., None], (LAYERS, 4, 2, 256, 128))

    stream = lax.all_to_all(tokens, COL, 1, 0, tiled=True).astype(f32)
    back = lax.all_to_all(cotangent, COL, 1, 0, tiled=True).astype(f32)
    stored = []
    for l in range(LAYERS):
        seen = core_gather(stream.astype(bf16))
        packed = seq_swap(run_qkv(weights[l], seen, b_qkv[l]))
        mixed, log = run_attend(packed)
        pair, blended = run_out(weights[l], here, seq_swap(mixed))
        attn_out = core_add(pair) + b_out[l][:, None]
        first, n_attn, i_attn = norm_forward(stream + attn_out, g_attn[l], s_attn[l])
        first_seen = core_gather(first.astype(bf16))
        pair, active, slope = run_ffn(weights[l], here, first_seen, b_up[l])
        lower = core_add(pair) + b_down[l][:, None]
        stream, n_ffn, i_ffn = norm_forward(first + lower, g_ffn[l], s_ffn[l])
        inputs = jnp.concatenate([active, first_seen, blended, seen], axis=0)
        inputs = lax.all_gather(inputs, X, axis=0, tiled=False)
        stored.append((inputs, packed, log, n_attn, i_attn, slope, n_ffn, i_ffn))
    result = lax.all_to_all(stream.astype(bf16), COL, 0, 1, tiled=True)

    minor = [None] * LAYERS
    for l in reversed(range(LAYERS)):
        (inputs, packed, log, n_attn, i_attn, slope, n_ffn, i_ffn) = stored[l]
        grad_sum = norm_backward(back, n_ffn, i_ffn, g_ffn[l])
        p_gain_ffn = jnp.sum(back * n_ffn, axis=1)
        p_shift_ffn = jnp.sum(back, axis=1)
        low = grad_sum.astype(bf16)
        p_down = jnp.sum(low.astype(f32), axis=1)
        pair, send_ud, p_up = run_ffn_back(weights[l], here, core_gather(low), slope)
        g_ud = lax.all_to_all(send_ud, X, 0, 0, tiled=True)
        if l == 0:
            rest = jnp.concatenate(
                [run_ffn_grad(after(late[0], send_ud), late[2]), run_attend_grad(after(late[1], send_ud), late[2])],
                axis=2,
            )
            rest = lax.psum_scatter(rest.reshape(16, 768, 128), ("y",) + Z, scatter_dimension=0)
            ud = reduce_stage(run_ffn_grad(g_ud, inputs).reshape(16, 512, 128), ("y",) + Z)
        grad_first = core_add(pair) + grad_sum
        p_gain_attn = jnp.sum(grad_first * n_attn, axis=1)
        p_shift_attn = jnp.sum(grad_first, axis=1)
        grad_total = norm_backward(grad_first, n_attn, i_attn, g_attn[l])
        low = grad_total.astype(bf16)
        p_out = jnp.sum(low.astype(f32), axis=1)
        low = core_gather(low)
        grad_blended = seq_swap(run_out_back(weights[l], low))
        grad_qkv = seq_swap(run_attend_back(packed, grad_blended, log))
        pair, send_qo, p_qkv = run_qkv_back(weights[l], here, grad_qkv, low)
        g_qo = lax.all_to_all(send_qo, X, 0, 0, tiled=True)
        if l == 1:
            late = (g_ud, g_qo, inputs)
        else:
            qo = reduce_stage(run_attend_grad(g_qo, inputs).reshape(16, 256, 128), ("y",) + Z)
        back = core_add(pair) + grad_total
        minor[l] = (p_qkv, p_out, p_gain_attn, p_shift_attn, p_down, p_gain_ffn, p_shift_ffn, p_up)
    rest = after(rest, send_qo).astype(f32)
    sums = ((ud[256:], ud[:256], qo), (rest[256:512], rest[:256], rest[512:]))
    swapped = trade(
        jnp.stack([jnp.concatenate([q[:192], u], axis=0) for _, u, q in sums]).astype(bf16)
    ).astype(f32)
    big = [
        (
            swapped[l, :192].reshape(3, 64, 128),
            sums[l][2][192:],
            swapped[l, 192:],
            sums[l][0].reshape(4, 64, 128).transpose(1, 0, 2).reshape(64, 512),
        )
        for l in range(LAYERS)
    ]
    grad_tokens = lax.all_to_all(back.astype(bf16), COL, 0, 1, tiled=True).astype(f32)

    mine = (jnp.arange(2) == core).astype(f32)
    qv = jnp.stack([m[0].reshape(4, 2, 3, 64)[:, :, ::2] for m in minor])
    qv = qv.transpose(1, 2, 0, 3, 4)
    qv = (qv[:, None] * mine[None, :, None, None, None, None]).reshape(16, 256)
    up = jnp.stack([m[7] for m in minor]).reshape(LAYERS, 4, 2, 256).transpose(1, 2, 0, 3)
    up = (up[:, None] * mine[None, :, None, None, None]).reshape(16, 512)
    feats = jnp.stack([jnp.stack([m[i] for m in minor]) for i in range(1, 7)])
    feats = feats.reshape(6, LAYERS, 16, 64).transpose(2, 0, 1, 3).reshape(16, 768)
    sums = jnp.concatenate([qv, feats, up], axis=1).reshape(4, 4, 12, 128)
    sums2 = sum_axis(reduce_stage(sums.reshape(16, 12, 128), COL), Y)
    sums2 = sums2 + lax.ppermute(sums2, CORE, [(0, 1), (1, 0)])
    flat = sums2.reshape(1536)
    o_qv = flat[:256].reshape(LAYERS, 2, 64)
    o_out, o_gain_attn, o_shift_attn, o_down, o_gain_ffn, o_shift_ffn = flat[256:1024].reshape(6, LAYERS, 64)
    o_up = flat[1024:].reshape(LAYERS, 256)
    gw_qkv, gw_out, gw_up, gw_down = [jnp.stack([b[i] for b in big]) for i in range(4)]
    return (
        result,
        grad_tokens,
        gw_qkv,
        o_qv,
        gw_out,
        o_out,
        o_gain_attn,
        o_shift_attn,
        gw_up,
        o_up,
        gw_down,
        o_down,
        o_gain_ffn,
        o_shift_ffn,
    )


def solution(mesh):
    fine = Mesh(mesh.devices.reshape(4, 2, 2, 2, 2, 2), ("y", "k", "xh", "xl", "zh", "zl"))
    row = ("y", "k")
    col = COL
    in_specs = (
        P(col, row),
        P(None, None, col, row),
        P(None, None, col),
        P(None, col, row),
        P(None, col),
        P(None, col),
        P(None, col),
        P(None, col, row),
        P(None, col),
        P(None, col, row),
        P(None, col),
        P(None, col),
        P(None, col),
        P(col, row),
    )
    out_specs = (
        P(col, row),
        P(col, row),
        P(None, None, col, row),
        P(None, None, col),
        P(None, col, row),
        P(None, col),
        P(None, col),
        P(None, col),
        P(None, col, row),
        P(None, col),
        P(None, col, row),
        P(None, col),
        P(None, col),
        P(None, col),
    )
    return jax.shard_map(
        on_device, mesh=fine, in_specs=in_specs, out_specs=out_specs, check_vma=False
    )
```

```python
from functools import partial
from typing import NamedTuple

import jax
import jax.numpy as jnp
from jax import lax
from jax.experimental import pallas as pl
from jax.experimental.pallas import tpu as pltpu
from jax.sharding import Mesh, PartitionSpec as P

HEAD = 64
D = 1024
LAYERS = 2
SEQ_LEN = 1024
epsilon = 1e-05

CORE = "k"
Y = ("y",)
X = ("xh", "xl")
Z = ("zh", "zl")
COL = X + Z
CHIPS = Y + COL
SEQ = ("xl", "zh", "zl")
bf16 = jnp.bfloat16
f32 = jnp.float32


NT = ((1,), (1,))
TN = ((0,), (0,))
NN = ((1,), (0,))


def mm(a, b, dims):
    return lax.dot_general(a, b, (dims, ((), ())), preferred_element_type=f32)


def core_gather(values):
    return lax.all_gather(values, CORE, axis=1, tiled=True)


def core_add(pair):
    keep, send = pair
    return keep + lax.ppermute(send, CORE, [(0, 1), (1, 0)]).astype(f32)


def trade(values):
    return lax.ppermute(values, (CORE, "zh"), [(0, 0), (1, 2), (2, 1), (3, 3)])


def pick(values, index, dim):
    return lax.dynamic_index_in_dim(values, index, dim, keepdims=False)


def reduce_stage(g, axes):
    return jnp.sum(lax.all_to_all(g, axes, 0, 0, tiled=True).astype(f32), axis=0)


SHIFTS = (0, 1, 3, 2)


def along(values, axes, shift):
    return lax.ppermute(values, axes, [(i, (i + shift) % 4) for i in range(4)])


def exchange(parts, axes):
    me = lax.axis_index(axes)
    return [pick(parts, me, 0)] + [along(pick(parts, (me + i) % 4, 0), axes, i) for i in SHIFTS[1:]]


def everyone(values, axes):
    return [values] + [along(values, axes, i) for i in SHIFTS[1:]]


def after(values, *others):
    return lax.optimization_barrier((values, *others))[0]


class Weights(NamedTuple):
    qo: jax.Array
    up: jax.Array
    down: jax.Array
    qo_at: int
    up_at: int
    down_at: int


def sum_axis(values, axes):
    total = values
    for shift in (1, 3, 2):
        total += lax.ppermute(values, axes, [(i, (i + shift) % 4) for i in range(4)])
    return total


def call(kernel, grid, ins, outs, scratch=(), flops=0, moved=0):
    return pl.pallas_call(
        kernel,
        grid=grid,
        in_specs=[spec for spec, _ in ins],
        out_specs=[spec for spec, _ in outs],
        out_shape=[shape for _, shape in outs],
        scratch_shapes=list(scratch),
        compiler_params=pltpu.CompilerParams(vmem_limit_bytes=50 * 1024 * 1024),
        cost_estimate=pl.CostEstimate(flops=flops, bytes_accessed=moved, transcendentals=0),
    )(*[value for _, value in ins])


def whole(value):
    rank = value.ndim
    return (pl.BlockSpec(value.shape, lambda g: (0,) * rank), value)


def scalar(value):
    return (pl.BlockSpec(memory_space=pltpu.SMEM), value)


def out_whole(shape, dtype):
    rank = len(shape)
    return (pl.BlockSpec(shape, lambda g: (0,) * rank), jax.ShapeDtypeStruct(shape, dtype))


def split_cores(core_ref, acc, keep_ref, send_ref):
    first = core_ref[0] == 0
    low, high = acc[:, :128], acc[:, 128:]
    keep_ref[...] = jnp.where(first, low, high)
    send_ref[...] = jnp.where(first, high, low).astype(bf16)


PAIR = (out_whole((D, 128), f32), out_whole((D, 128), bf16))


def w_qkv_spec(i):
    return pl.BlockSpec((4, 1, 2, 2, 256, 128), lambda g: (0, g, 0, 0, i, 0))


def w_out_spec(i):
    return pl.BlockSpec((4, 4, 2, 2, 64, 128), lambda g: (0, 0, 0, 0, 4 * i + 3, 0))


def w_up_spec(i):
    return pl.BlockSpec((4, 1, 2, 2, 256, 128), lambda g: (0, g, 0, 0, i, 0))


def w_down_spec(i):
    return pl.BlockSpec((1, 4, 2, 2, 256, 128), lambda g: (g, 0, 0, 0, i, 0))


def rows_by_inputs(w_ref, b, rows=256):
    return jnp.concatenate([w_ref[y, 0, a, b, :rows] for y in range(4) for a in range(2)], axis=1)


def down_block(w_ref):
    rows = []
    for x in range(4):
        for a in range(2):
            for b in range(2):
                blk = w_ref[0, x, a, b]
                rows.append(jnp.concatenate([blk[j * 64 : (j + 1) * 64] for j in range(4)], axis=1))
    return jnp.concatenate(rows, axis=0)


def out_block(w_ref):
    rows = []
    for x in range(4):
        for a in range(2):
            for b in range(2):
                rows.append(jnp.concatenate([w_ref[y, x, a, b] for y in range(4)], axis=1))
    return jnp.concatenate(rows, axis=0)


def qkv_kernel(w_ref, x_ref, bias_ref, o_ref):
    x = x_ref[...]
    for b in range(2):
        r = mm(rows_by_inputs(w_ref, b, 192), x, NN)
        for s in range(2):
            v = (r[:, s * 128 : (s + 1) * 128] + bias_ref[0, b]).astype(bf16)
            for j in range(3):
                o_ref[s, 0, j * 128 + b * 64 : j * 128 + b * 64 + 64, :] = v[j * 64 : (j + 1) * 64]


def run_qkv(w, seen, bias):
    out = call(
        qkv_kernel,
        (4,),
        [
            (w_qkv_spec(w.qo_at), w.qo),
            whole(seen),
            (pl.BlockSpec((1, 2, 192, 128), lambda g: (g, 0, 0, 0)), bias),
        ],
        [
            (
                pl.BlockSpec((2, 1, 384, 128), lambda g: (0, g, 0, 0)),
                jax.ShapeDtypeStruct((2, 4, 384, 128), bf16),
            )
        ],
        flops=2 * 1536 * 1024 * 256,
        moved=5 << 20,
    )[0]
    return out.reshape(8, 384, 128)


def join_heads(ref, rows):
    return jnp.concatenate(
        [jnp.concatenate([ref[s * 4 + h] for h in range(4)], axis=0) for s in range(2)], axis=1
    )


def out_kernel(core_ref, w_ref, b_ref, keep_ref, send_ref, blended_ref):
    blended = join_heads(b_ref, 128)
    blended_ref[...] = blended
    split_cores(core_ref, mm(out_block(w_ref), blended, NN), keep_ref, send_ref)


def run_out(w, core, arrived):
    keep, send, blended = call(
        out_kernel,
        (1,),
        [scalar(core), (w_out_spec(w.qo_at), w.qo), whole(arrived)],
        [*PAIR, out_whole((512, 256), bf16)],
        flops=2 * 1024 * 512 * 256,
        moved=2 << 20,
    )
    return (keep, send), blended


def ffn_kernel(core_ref, up_ref, down_ref, x_ref, bias_ref, keep_ref, send_ref, act_ref, slope_ref, acc):
    g = pl.program_id(0)
    x = x_ref[...]
    acts = []
    for b in range(2):
        r = mm(rows_by_inputs(up_ref, b), x, NN)
        bias = bias_ref[0, b]
        r = r + jnp.concatenate([bias, bias], axis=1)
        half = 0.5 * (1.0 + lax.erf(r * (2.0**-0.5)))
        act = (r * half).astype(bf16)
        slope_ref[b * 256 : (b + 1) * 256, :] = half + r * jnp.exp(-0.5 * r * r) * 0.3989422804014327
        act_ref[b * 256 : (b + 1) * 256, :] = act
        acts.append(act)
    part = mm(down_block(down_ref), jnp.concatenate(acts, axis=0), NN)

    @pl.when(g == 0)
    def _():
        acc[...] = part

    @pl.when(g > 0)
    def _():
        acc[...] += part

    @pl.when(g == 3)
    def _():
        split_cores(core_ref, acc[...], keep_ref, send_ref)


def by_step(rows, columns):
    return pl.BlockSpec((rows, columns), lambda g: (g, 0))


def run_ffn(w, core, seen, bias):
    keep, send, act, slope = call(
        ffn_kernel,
        (4,),
        [
            scalar(core),
            (w_up_spec(w.up_at), w.up),
            (w_down_spec(w.down_at), w.down),
            whole(seen),
            (pl.BlockSpec((1, 2, 256, 128), lambda g: (g, 0, 0, 0)), bias),
        ],
        [
            *PAIR,
            (by_step(512, 256), jax.ShapeDtypeStruct((2048, 256), bf16)),
            (by_step(512, 256), jax.ShapeDtypeStruct((2048, 256), f32)),
        ],
        [pltpu.VMEM((D, 256), f32)],
        flops=4 * 2048 * 1024 * 256,
        moved=13 << 20,
    )
    return (keep, send), act, slope


def ffn_back_kernel(core_ref, up_ref, down_ref, low_ref, slope_ref, keep_ref, send_ref, bias_ref, g_ref, acc):
    g = pl.program_id(0)
    low = low_ref[...]
    gu = (mm(down_block(down_ref), low, TN) * slope_ref[...]).astype(bf16)
    bias_ref[...] = jnp.sum(gu.astype(f32), axis=1, keepdims=True)
    g_ref[0] = gu
    up = jnp.concatenate([rows_by_inputs(up_ref, b) for b in range(2)], axis=0)
    part = mm(up, gu, TN)

    @pl.when(g == 0)
    def _():
        acc[...] = part

    @pl.when(g > 0)
    def _():
        acc[...] += part

    @pl.when(g == 3)
    def _():
        split_cores(core_ref, acc[...], keep_ref, send_ref)


def run_ffn_back(w, core, low, slope):
    keep, send, bias, grads = call(
        ffn_back_kernel,
        (4,),
        [
            scalar(core),
            (w_up_spec(w.up_at), w.up),
            (w_down_spec(w.down_at), w.down),
            whole(low),
            (by_step(512, 256), slope),
        ],
        [
            *PAIR,
            (by_step(512, 1), jax.ShapeDtypeStruct((2048, 1), f32)),
            (pl.BlockSpec((1, 512, 256), lambda g: (g, 0, 0)), jax.ShapeDtypeStruct((4, 512, 256), bf16)),
        ],
        [pltpu.VMEM((D, 256), f32)],
        flops=4 * 2048 * 1024 * 256,
        moved=14 << 20,
    )
    return (keep, send), grads, bias


def wide(refs, top, rows):
    return jnp.concatenate([ref[top : top + rows] for ref in refs], axis=1)


def from_chips(src_ref, refs):
    if len(refs) == 4:
        return jnp.concatenate([ref[...] for ref in refs], axis=1)
    return jnp.concatenate([refs[0][src_ref[i]] for i in range(4)], axis=1)


def down_grad_kernel(*refs):
    o_ref = refs[-1]
    gd = mm(wide(refs[:4], 0, 256), jnp.concatenate([ref[0] for ref in refs[4:8]], axis=1), NT).astype(bf16)
    for z in range(4):
        for j in range(4):
            o_ref[0, z, j * 64 : (j + 1) * 64, :] = gd[z * 64 : (z + 1) * 64, j * 128 : (j + 1) * 128]


def run_down_grad(l, low, active):
    return call(
        down_grad_kernel,
        (4,),
        [*[(by_step(256, 256), v) for v in low], *[(pl.BlockSpec((1, 512, 256), lambda g: (l, 0, 0)), v) for v in active]],
        [(pl.BlockSpec((1, 4, 256, 128), lambda g: (g, 0, 0, 0)), jax.ShapeDtypeStruct((4, 4, 256, 128), bf16))],
        flops=2 * 1024 * 1024 * 512,
        moved=6 << 20,
    )[0]


def up_grad_kernel(src_ref, *refs):
    o_ref = refs[-1]
    gu = mm(wide(refs[:4], 0, 512), from_chips(src_ref, refs[4:-1]), NT).astype(bf16)
    for a in range(2):
        for b in range(2):
            o_ref[0, a * 2 + b] = gu[b * 256 : (b + 1) * 256, a * 128 : (a + 1) * 128]


def attend_grad_kernel(top, src_ref, *refs):
    o_ref = refs[-1]
    g_refs, others = refs[:4], refs[4:-1]
    half = len(others) // 2
    go = mm(wide(g_refs, top, 256), from_chips(src_ref, others[:half]), NT).astype(bf16)
    gq = mm(wide(g_refs, top + 256, 384), from_chips(src_ref, others[half:]), NT).astype(bf16)
    for a in range(2):
        for b in range(2):
            z = a * 2 + b
            for j in range(3):
                at = j * 128 + b * 64
                o_ref[0, z, j * 64 : (j + 1) * 64, :] = gq[at : at + 64, a * 128 : (a + 1) * 128]
            o_ref[0, z, 192:256, :] = go[z * 64 : (z + 1) * 64]


def inputs_specs(inputs, rows, base):
    if isinstance(inputs, list):
        return [(pl.BlockSpec((rows, 256), lambda g: (base + g, 0)), v) for v in inputs]
    return [(pl.BlockSpec((4, rows, 256), lambda g: (0, base + g, 0)), inputs)]


def run_grad(kernel, src, arrived, inputs, *specs):
    return call(
        kernel,
        (4,),
        [
            scalar(src),
            *[whole(v) for v in arrived],
            *[one for spec in specs for one in inputs_specs(inputs, *spec)],
        ],
        [(pl.BlockSpec((1, 4, 256, 128), lambda g: (g, 0, 0, 0)), jax.ShapeDtypeStruct((4, 4, 256, 128), bf16))],
        flops=2 * 1024 * 1024 * 512,
        moved=6 << 20,
    )[0]


def run_up_grad(src, arrived, inputs):
    return run_grad(up_grad_kernel, src, arrived, inputs, (256, 0))


def run_attend_grad(top, src, arrived, inputs):
    return run_grad(partial(attend_grad_kernel, top), src, arrived, inputs, (128, 8), (256, 6))


def out_back_kernel(w_ref, low_ref, o_ref):
    r = mm(out_block(w_ref), low_ref[...], TN).astype(bf16)
    for s in range(2):
        for h in range(4):
            o_ref[s * 4 + h] = r[h * 128 : (h + 1) * 128, s * 128 : (s + 1) * 128]


def run_out_back(w, low):
    return call(
        out_back_kernel,
        (1,),
        [(w_out_spec(w.qo_at), w.qo), whole(low)],
        [out_whole((8, 128, 128), bf16)],
        flops=2 * 1024 * 512 * 256,
        moved=2 << 20,
    )[0]


def qkv_back_kernel(core_ref, w_ref, gq_ref, low_ref, keep_ref, send_ref, g_ref, bias_ref, acc):
    g = pl.program_id(0)
    both = jnp.concatenate([gq_ref[0, 0], gq_ref[1, 0]], axis=1)
    g_ref[0, 0:256] = low_ref[...]
    g_ref[0, 256:640] = both
    part = None
    for b in range(2):
        gq = jnp.concatenate([both[j * 128 + b * 64 : j * 128 + b * 64 + 64] for j in range(3)], axis=0)
        bias_ref[0, b] = jnp.sum(gq.astype(f32), axis=1, keepdims=True)
        term = mm(rows_by_inputs(w_ref, b, 192), gq, TN)
        part = term if part is None else part + term

    @pl.when(g == 0)
    def _():
        acc[...] = part

    @pl.when(g > 0)
    def _():
        acc[...] += part

    @pl.when(g == 3)
    def _():
        split_cores(core_ref, acc[...], keep_ref, send_ref)


def run_qkv_back(w, core, arrived, low):
    keep, send, grads, bias = call(
        qkv_back_kernel,
        (4,),
        [
            scalar(core),
            (w_qkv_spec(w.qo_at), w.qo),
            (pl.BlockSpec((2, 1, 384, 128), lambda g: (0, g, 0, 0)), arrived.reshape(2, 4, 384, 128)),
            (by_step(256, 256), low),
        ],
        [
            *PAIR,
            (pl.BlockSpec((1, 640, 256), lambda g: (g, 0, 0)), jax.ShapeDtypeStruct((4, 640, 256), bf16)),
            (pl.BlockSpec((1, 2, 192, 1), lambda g: (g, 0, 0, 0)), jax.ShapeDtypeStruct((4, 2, 192, 1), f32)),
        ],
        [pltpu.VMEM((D, 256), f32)],
        flops=2 * 1536 * 1024 * 256,
        moved=7 << 20,
    )
    return (keep, send), grads, bias


FACTOR = HEAD ** (-0.5)
STEP = 256


def join_tokens(ref, top):
    return jnp.concatenate([ref[c, top : top + HEAD] for c in range(8)], axis=1)


def attend_kernel(p_ref, o_ref, log_ref):
    for h in range(2):
        q = join_tokens(p_ref, h * 64)
        k = join_tokens(p_ref, 128 + h * 64)
        v = join_tokens(p_ref, 256 + h * 64)
        for c in range(SEQ_LEN // STEP):
            scores = mm(k, q[:, c * STEP : (c + 1) * STEP], TN) * FACTOR
            highest = jnp.max(scores, axis=0, keepdims=True)
            exps = jnp.exp(scores - highest)
            total = jnp.sum(exps, axis=0, keepdims=True)
            low = (exps * (1.0 / total)).astype(bf16)
            out = mm(v, low, NN).astype(bf16)
            log_ref[h : h + 1, c * STEP : (c + 1) * STEP] = highest + jnp.log(total)
            for n in range(STEP // 128):
                o_ref[c * (STEP // 128) + n, h * 64 : h * 64 + 64, :] = out[:, n * 128 : (n + 1) * 128]


def run_attend(packed):
    return call(
        attend_kernel,
        (1,),
        [whole(packed)],
        [out_whole((8, 128, 128), bf16), out_whole((2, SEQ_LEN), f32)],
        flops=8 * 1024 * 1024 * 128,
        moved=1 << 20,
    )


def attend_back_kernel(p_ref, b_ref, log_ref, o_ref):
    for h in range(2):
        q = join_tokens(p_ref, h * 64)
        k = join_tokens(p_ref, 128 + h * 64)
        v = join_tokens(p_ref, 256 + h * 64)
        gb = join_tokens(b_ref, h * 64)
        gk = gv = None
        for c in range(SEQ_LEN // STEP):
            cols = slice(c * STEP, (c + 1) * STEP)
            qc, gc = q[:, cols], gb[:, cols]
            probs = jnp.exp(mm(k, qc, TN) * FACTOR - log_ref[h : h + 1, cols])
            gp = mm(v, gc, TN)
            row = jnp.sum(probs * gp, axis=0, keepdims=True)
            ds = (probs * (gp - row)).astype(bf16)
            tv = mm(gc, probs.astype(bf16), NT)
            tk = mm(qc, ds, NT)
            gv = tv if gv is None else gv + tv
            gk = tk if gk is None else gk + tk
            gq = (mm(k, ds, NN) * FACTOR).astype(bf16)
            for n in range(STEP // 128):
                o_ref[c * (STEP // 128) + n, h * 64 : h * 64 + 64, :] = gq[:, n * 128 : (n + 1) * 128]
        gk = (gk * FACTOR).astype(bf16)
        gv = gv.astype(bf16)
        for c in range(8):
            o_ref[c, 128 + h * 64 : 192 + h * 64, :] = gk[:, c * 128 : (c + 1) * 128]
            o_ref[c, 256 + h * 64 : 320 + h * 64, :] = gv[:, c * 128 : (c + 1) * 128]


def run_attend_back(packed, grad, log):
    return call(
        attend_back_kernel,
        (1,),
        [whole(packed), whole(grad), whole(log)],
        [out_whole((8, 384, 128), bf16)],
        flops=20 * 1024 * 1024 * 128,
        moved=2 << 20,
    )[0]


def seq_swap(values):
    return lax.all_to_all(values, SEQ, 0, 0, tiled=True)


def norm_forward(summed, gain, shift):
    centre = jnp.mean(summed, axis=0, keepdims=True)
    centred = summed - centre
    variance = jnp.mean(centred * centred, axis=0, keepdims=True)
    scaled = lax.rsqrt(variance + epsilon)
    normed = centred * scaled
    return normed * gain[:, None] + shift[:, None], normed, scaled


def norm_backward(incoming, normed, scaled, gain):
    grad_norm = incoming * gain[:, None]
    plain = jnp.mean(grad_norm, axis=0, keepdims=True)
    cross = jnp.mean(grad_norm * normed, axis=0, keepdims=True)
    return scaled * (grad_norm - plain - normed * cross)


def on_device(
    tokens,
    w_qkv,
    bias_qv,
    w_out,
    bias_out,
    gain_attn,
    shift_attn,
    w_up,
    bias_up,
    w_down,
    bias_down,
    gain_ffn,
    shift_ffn,
    cotangent,
):
    core = lax.axis_index(CORE)
    here = core.astype(jnp.int32).reshape(1)
    src = jnp.stack([(lax.axis_index(X) - i) % 4 for i in SHIFTS]).astype(jnp.int32)
    traded = trade(
        jnp.concatenate([w_qkv.reshape(LAYERS, 192, 128), w_up.reshape(LAYERS, 256, 128)], axis=1)
    )
    pack = jnp.concatenate(
        [
            traded[:, :192],
            w_out,
            traded[:, 192:],
            w_down.reshape(LAYERS, 64, 4, 128).transpose(0, 2, 1, 3).reshape(LAYERS, 256, 128),
        ],
        axis=1,
    )
    head = jnp.concatenate([pack[0], pack[1, :256]], axis=0)
    head = lax.all_gather(head, CHIPS, axis=0, tiled=False).reshape(4, 4, 2, 2, 1024, 128)
    tail = lax.all_gather(pack[1, 256:], CHIPS, axis=0, tiled=False).reshape(4, 4, 2, 2, 512, 128)
    weights = (Weights(head, head, head, 0, 1, 2), Weights(head, tail, tail, 3, 0, 1))

    small = jnp.concatenate(
        [
            v.reshape(-1)
            for v in (bias_qv, bias_out, gain_attn, shift_attn, bias_down, gain_ffn, shift_ffn, bias_up)
        ]
    )
    small = lax.all_to_all(
        jnp.broadcast_to(small[None], (16, small.shape[0])), COL, 0, 0, tiled=True
    )
    b_qv = small[:, :256].reshape(4, 2, 2, LAYERS, 2, 64)
    b_qv = pick(b_qv, core, 1).transpose(2, 0, 1, 3, 4)
    b_qkv = jnp.stack([b_qv[:, :, :, 0], jnp.zeros_like(b_qv[:, :, :, 0]), b_qv[:, :, :, 1]], axis=3)
    b_qkv = jnp.broadcast_to(b_qkv.reshape(LAYERS, 4, 2, 192, 1), (LAYERS, 4, 2, 192, 128))
    features = small[:, 256:1024].reshape(16, 6, LAYERS, 64).transpose(1, 2, 0, 3).reshape(6, LAYERS, D)
    b_out, g_attn, s_attn, b_down, g_ffn, s_ffn = features
    b_up = small[:, 1024:].reshape(4, 2, 2, LAYERS, 256)
    b_up = pick(b_up, core, 1).transpose(2, 0, 1, 3)
    b_up = jnp.broadcast_to(b_up[..., None], (LAYERS, 4, 2, 256, 128))

    stream = lax.all_to_all(tokens, COL, 1, 0, tiled=True).astype(f32)
    back = lax.all_to_all(cotangent, COL, 1, 0, tiled=True).astype(f32)
    stream, back = lax.optimization_barrier((stream, back))
    stored = []
    for l in range(LAYERS):
        seen = core_gather(stream.astype(bf16))
        packed = seq_swap(run_qkv(weights[l], seen, b_qkv[l]))
        mixed, log = run_attend(packed)
        pair, blended = run_out(weights[l], here, seq_swap(mixed))
        attn_out = core_add(pair) + b_out[l][:, None]
        first, n_attn, i_attn = norm_forward(stream + attn_out, g_attn[l], s_attn[l])
        first_seen = core_gather(first.astype(bf16))
        pair, active, slope = run_ffn(weights[l], here, first_seen, b_up[l])
        lower = core_add(pair) + b_down[l][:, None]
        stream, n_ffn, i_ffn = norm_forward(first + lower, g_ffn[l], s_ffn[l])
        inputs = jnp.concatenate([first_seen, blended, seen], axis=0)
        inputs = lax.all_gather(inputs, X, axis=0, tiled=False)
        stored.append((inputs, active, packed, log, n_attn, i_attn, slope, n_ffn, i_ffn))
    result = stream.astype(bf16)
    active = jnp.stack([kept[1].reshape(4, 512, 256) for kept in stored], axis=1)
    active = exchange(active, Y)

    minor = [None] * LAYERS
    for l in reversed(range(LAYERS)):
        (inputs, _, packed, log, n_attn, i_attn, slope, n_ffn, i_ffn) = stored[l]
        grad_sum = norm_backward(back, n_ffn, i_ffn, g_ffn[l])
        p_gain_ffn = jnp.sum(back * n_ffn, axis=1)
        p_shift_ffn = jnp.sum(back, axis=1)
        low = grad_sum.astype(bf16)
        p_down = jnp.sum(low.astype(f32), axis=1)
        low = core_gather(low)
        g_down = everyone(low, Y)
        pair, send_up, p_up = run_ffn_back(weights[l], here, low, slope)
        if l == 0:
            g_up = exchange(send_up, X)
        if l == 0:
            late = after(late, send_up)
            downs = jnp.stack(
                [run_down_grad(0, g_down, active), run_down_grad(1, late[0], active)], axis=2
            )
            rest = jnp.concatenate(
                [run_up_grad(src, late[1], late[2]), run_attend_grad(512, src, late[1], late[2])], axis=2
            )
        grad_first = core_add(pair) + grad_sum
        p_gain_attn = jnp.sum(grad_first * n_attn, axis=1)
        p_shift_attn = jnp.sum(grad_first, axis=1)
        grad_total = norm_backward(grad_first, n_attn, i_attn, g_attn[l])
        low = grad_total.astype(bf16)
        p_out = jnp.sum(low.astype(f32), axis=1)
        low = core_gather(low)
        grad_blended = seq_swap(run_out_back(weights[l], low))
        grad_qkv = seq_swap(run_attend_back(packed, grad_blended, log))
        if l == 0:
            low, downs, rest, up_0 = lax.optimization_barrier(
                (low, downs, rest, run_up_grad(src, g_up, inputs))
            )
            rest = lax.psum_scatter(rest.reshape(16, 512, 128), ("y",) + Z, scatter_dimension=0)
            downs = reduce_stage(downs.reshape(16, 512, 128), COL)
        pair, send_qo, p_qkv = run_qkv_back(weights[l], here, grad_qkv, low)
        if l == 1:
            late = (g_down, exchange(jnp.concatenate([send_up, send_qo], axis=1), X), inputs)
        else:
            send_qo = after(send_qo, downs)
            g_qo = exchange(send_qo, X)
            first = jnp.concatenate(
                [up_0, run_attend_grad(0, src, g_qo, inputs)], axis=2
            )
            pair = after(pair, first)
            first = reduce_stage(first.reshape(16, 512, 128), ("y",) + Z)
        back = core_add(pair) + grad_total
        minor[l] = (p_qkv, p_out, p_gain_attn, p_shift_attn, p_down, p_gain_ffn, p_shift_ffn, p_up)
    rest = after(rest, send_qo).astype(f32)
    sums = ((downs[:256], first[:256], first[256:]), (downs[256:], rest[:256], rest[256:]))
    swapped = trade(
        jnp.stack([jnp.concatenate([q[:192], u], axis=0) for _, u, q in sums]).astype(bf16)
    ).astype(f32)
    big = [
        (
            swapped[l, :192].reshape(3, 64, 128),
            sums[l][2][192:],
            swapped[l, 192:],
            sums[l][0].reshape(4, 64, 128).transpose(1, 0, 2).reshape(64, 512),
        )
        for l in range(LAYERS)
    ]
    mine = (jnp.arange(2) == core).astype(f32)
    qv = jnp.stack([m[0].reshape(4, 2, 3, 64)[:, :, ::2] for m in minor])
    qv = qv.transpose(1, 2, 0, 3, 4)
    qv = (qv[:, None] * mine[None, :, None, None, None, None]).reshape(16, 256)
    up = jnp.stack([m[7] for m in minor]).reshape(LAYERS, 4, 2, 256).transpose(1, 2, 0, 3)
    up = (up[:, None] * mine[None, :, None, None, None]).reshape(16, 512)
    feats = jnp.stack([jnp.stack([m[i] for m in minor]) for i in range(1, 7)])
    feats = feats.reshape(6, LAYERS, 16, 64).transpose(2, 0, 1, 3).reshape(16, 768)
    sums = jnp.concatenate([qv, feats, up], axis=1).reshape(16, 12, 128)
    high = sums.astype(bf16)
    low = (sums - high.astype(f32)).astype(bf16)
    send = jnp.concatenate([result.reshape(16, 64, 128), back.astype(bf16).reshape(16, 64, 128), high, low], axis=1)
    got = lax.all_to_all(send, COL, 0, 0, tiled=True)
    result = got[:, :64].transpose(1, 0, 2).reshape(64, 2048)
    grad_tokens = got[:, 64:128].astype(f32).transpose(1, 0, 2).reshape(64, 2048)
    sums2 = jnp.sum(got[:, 128:140].astype(f32), axis=0) + jnp.sum(got[:, 140:].astype(f32), axis=0)
    sums2 = sum_axis(sums2, Y)
    sums2 = sums2 + lax.ppermute(sums2, CORE, [(0, 1), (1, 0)])
    flat = sums2.reshape(1536)
    o_qv = flat[:256].reshape(LAYERS, 2, 64)
    o_out, o_gain_attn, o_shift_attn, o_down, o_gain_ffn, o_shift_ffn = flat[256:1024].reshape(6, LAYERS, 64)
    o_up = flat[1024:].reshape(LAYERS, 256)
    gw_qkv, gw_out, gw_up, gw_down = [jnp.stack([b[i] for b in big]) for i in range(4)]
    return (
        result,
        grad_tokens,
        gw_qkv,
        o_qv,
        gw_out,
        o_out,
        o_gain_attn,
        o_shift_attn,
        gw_up,
        o_up,
        gw_down,
        o_down,
        o_gain_ffn,
        o_shift_ffn,
    )


def solution(mesh):
    fine = Mesh(mesh.devices.reshape(4, 2, 2, 2, 2, 2), ("y", "k", "xh", "xl", "zh", "zl"))
    row = ("y", "k")
    col = COL
    in_specs = (
        P(col, row),
        P(None, None, col, row),
        P(None, None, col),
        P(None, col, row),
        P(None, col),
        P(None, col),
        P(None, col),
        P(None, col, row),
        P(None, col),
        P(None, col, row),
        P(None, col),
        P(None, col),
        P(None, col),
        P(col, row),
    )
    out_specs = (
        P(col, row),
        P(col, row),
        P(None, None, col, row),
        P(None, None, col),
        P(None, col, row),
        P(None, col),
        P(None, col),
        P(None, col),
        P(None, col, row),
        P(None, col),
        P(None, col, row),
        P(None, col),
        P(None, col),
        P(None, col),
    )
    return jax.shard_map(
        on_device, mesh=fine, in_specs=in_specs, out_specs=out_specs, check_vma=False
    )
```

```python
from functools import partial
from typing import NamedTuple

import jax
import jax.numpy as jnp
from jax import lax
from jax.experimental import pallas as pl
from jax.experimental.pallas import tpu as pltpu
from jax.sharding import Mesh, PartitionSpec as P

HEAD = 64
D = 1024
LAYERS = 2
SEQ_LEN = 1024
epsilon = 1e-05

CORE = "k"
Y = ("y",)
X = ("xh", "xl")
Z = ("zh", "zl")
COL = X + Z
CHIPS = Y + COL
SEQ = ("xl", "zh", "zl")
bf16 = jnp.bfloat16
f32 = jnp.float32


NT = ((1,), (1,))
TN = ((0,), (0,))
NN = ((1,), (0,))


def mm(a, b, dims):
    return lax.dot_general(a, b, (dims, ((), ())), preferred_element_type=f32)


def core_gather(values):
    return lax.all_gather(values, CORE, axis=1, tiled=True)


def core_add(pair):
    keep, send = pair
    return keep + lax.ppermute(send, CORE, [(0, 1), (1, 0)]).astype(f32)


def trade(values):
    return lax.ppermute(values, (CORE, "zh"), [(0, 0), (1, 2), (2, 1), (3, 3)])


def pick(values, index, dim):
    return lax.dynamic_index_in_dim(values, index, dim, keepdims=False)


def reduce_stage(g, axes):
    return jnp.sum(lax.all_to_all(g, axes, 0, 0, tiled=True).astype(f32), axis=0)


SHIFTS = (0, 1, 3, 2)


def along(values, axes, shift):
    return lax.ppermute(values, axes, [(i, (i + shift) % 4) for i in range(4)])


def exchange(parts, axes):
    me = lax.axis_index(axes)
    return [pick(parts, me, 0)] + [along(pick(parts, (me + i) % 4, 0), axes, i) for i in SHIFTS[1:]]


def everyone(values, axes):
    return [values] + [along(values, axes, i) for i in SHIFTS[1:]]


def after(values, *others):
    return lax.optimization_barrier((values, *others))[0]


class Weights(NamedTuple):
    qo: jax.Array
    up: jax.Array
    down: jax.Array
    qo_at: int
    up_at: int
    down_at: int


def sum_axis(values, axes):
    total = values
    for shift in (1, 3, 2):
        total += lax.ppermute(values, axes, [(i, (i + shift) % 4) for i in range(4)])
    return total


def call(kernel, grid, ins, outs, scratch=(), flops=0, moved=0):
    return pl.pallas_call(
        kernel,
        grid=grid,
        in_specs=[spec for spec, _ in ins],
        out_specs=[spec for spec, _ in outs],
        out_shape=[shape for _, shape in outs],
        scratch_shapes=list(scratch),
        compiler_params=pltpu.CompilerParams(vmem_limit_bytes=50 * 1024 * 1024),
        cost_estimate=pl.CostEstimate(flops=flops, bytes_accessed=moved, transcendentals=0),
    )(*[value for _, value in ins])


def whole(value):
    rank = value.ndim
    return (pl.BlockSpec(value.shape, lambda g: (0,) * rank), value)


def scalar(value):
    return (pl.BlockSpec(memory_space=pltpu.SMEM), value)


def out_whole(shape, dtype):
    rank = len(shape)
    return (pl.BlockSpec(shape, lambda g: (0,) * rank), jax.ShapeDtypeStruct(shape, dtype))


def split_cores(core_ref, acc, keep_ref, send_ref):
    first = core_ref[0] == 0
    low, high = acc[:, :128], acc[:, 128:]
    keep_ref[...] = jnp.where(first, low, high)
    send_ref[...] = jnp.where(first, high, low).astype(bf16)


PAIR = (out_whole((D, 128), f32), out_whole((D, 128), bf16))


def w_qkv_spec(i):
    return pl.BlockSpec((4, 1, 2, 2, 256, 128), lambda g: (0, g, 0, 0, i, 0))


def w_out_spec(i):
    return pl.BlockSpec((4, 4, 2, 2, 64, 128), lambda g: (0, 0, 0, 0, 4 * i + 3, 0))


def w_up_spec(i):
    return pl.BlockSpec((4, 1, 2, 2, 256, 128), lambda g: (0, g, 0, 0, i, 0))


def w_down_spec(i):
    return pl.BlockSpec((1, 4, 2, 2, 256, 128), lambda g: (g, 0, 0, 0, i, 0))


def rows_by_inputs(w_ref, b, rows=256):
    return jnp.concatenate([w_ref[y, 0, a, b, :rows] for y in range(4) for a in range(2)], axis=1)


def down_block(w_ref):
    rows = []
    for x in range(4):
        for a in range(2):
            for b in range(2):
                blk = w_ref[0, x, a, b]
                rows.append(jnp.concatenate([blk[j * 64 : (j + 1) * 64] for j in range(4)], axis=1))
    return jnp.concatenate(rows, axis=0)


def out_block(w_ref):
    rows = []
    for x in range(4):
        for a in range(2):
            for b in range(2):
                rows.append(jnp.concatenate([w_ref[y, x, a, b] for y in range(4)], axis=1))
    return jnp.concatenate(rows, axis=0)


def qkv_kernel(w_ref, x_ref, bias_ref, o_ref):
    x = x_ref[...]
    for b in range(2):
        r = mm(rows_by_inputs(w_ref, b, 192), x, NN)
        for s in range(2):
            v = (r[:, s * 128 : (s + 1) * 128] + bias_ref[0, b]).astype(bf16)
            for j in range(3):
                o_ref[s, 0, j * 128 + b * 64 : j * 128 + b * 64 + 64, :] = v[j * 64 : (j + 1) * 64]


def run_qkv(w, seen, bias):
    out = call(
        qkv_kernel,
        (4,),
        [
            (w_qkv_spec(w.qo_at), w.qo),
            whole(seen),
            (pl.BlockSpec((1, 2, 192, 128), lambda g: (g, 0, 0, 0)), bias),
        ],
        [
            (
                pl.BlockSpec((2, 1, 384, 128), lambda g: (0, g, 0, 0)),
                jax.ShapeDtypeStruct((2, 4, 384, 128), bf16),
            )
        ],
        flops=2 * 1536 * 1024 * 256,
        moved=5 << 20,
    )[0]
    return out.reshape(8, 384, 128)


def join_heads(ref, rows):
    return jnp.concatenate(
        [jnp.concatenate([ref[s * 4 + h] for h in range(4)], axis=0) for s in range(2)], axis=1
    )


def out_kernel(core_ref, w_ref, b_ref, keep_ref, send_ref, blended_ref):
    blended = join_heads(b_ref, 128)
    blended_ref[...] = blended
    split_cores(core_ref, mm(out_block(w_ref), blended, NN), keep_ref, send_ref)


def run_out(w, core, arrived):
    keep, send, blended = call(
        out_kernel,
        (1,),
        [scalar(core), (w_out_spec(w.qo_at), w.qo), whole(arrived)],
        [*PAIR, out_whole((512, 256), bf16)],
        flops=2 * 1024 * 512 * 256,
        moved=2 << 20,
    )
    return (keep, send), blended


def ffn_kernel(core_ref, up_ref, down_ref, x_ref, bias_ref, keep_ref, send_ref, act_ref, slope_ref, acc):
    g = pl.program_id(0)
    x = x_ref[...]
    acts = []
    for b in range(2):
        r = mm(rows_by_inputs(up_ref, b), x, NN)
        bias = bias_ref[0, b]
        r = r + jnp.concatenate([bias, bias], axis=1)
        half = 0.5 * (1.0 + lax.erf(r * (2.0**-0.5)))
        act = (r * half).astype(bf16)
        slope_ref[b * 256 : (b + 1) * 256, :] = half + r * jnp.exp(-0.5 * r * r) * 0.3989422804014327
        act_ref[b * 256 : (b + 1) * 256, :] = act
        acts.append(act)
    part = mm(down_block(down_ref), jnp.concatenate(acts, axis=0), NN)

    @pl.when(g == 0)
    def _():
        acc[...] = part

    @pl.when(g > 0)
    def _():
        acc[...] += part

    @pl.when(g == 3)
    def _():
        split_cores(core_ref, acc[...], keep_ref, send_ref)


def by_step(rows, columns):
    return pl.BlockSpec((rows, columns), lambda g: (g, 0))


def run_ffn(w, core, seen, bias):
    keep, send, act, slope = call(
        ffn_kernel,
        (4,),
        [
            scalar(core),
            (w_up_spec(w.up_at), w.up),
            (w_down_spec(w.down_at), w.down),
            whole(seen),
            (pl.BlockSpec((1, 2, 256, 128), lambda g: (g, 0, 0, 0)), bias),
        ],
        [
            *PAIR,
            (by_step(512, 256), jax.ShapeDtypeStruct((2048, 256), bf16)),
            (by_step(512, 256), jax.ShapeDtypeStruct((2048, 256), f32)),
        ],
        [pltpu.VMEM((D, 256), f32)],
        flops=4 * 2048 * 1024 * 256,
        moved=13 << 20,
    )
    return (keep, send), act, slope


def ffn_back_kernel(core_ref, up_ref, down_ref, low_ref, slope_ref, keep_ref, send_ref, bias_ref, g_ref, acc):
    g = pl.program_id(0)
    low = low_ref[...]
    gu = (mm(down_block(down_ref), low, TN) * slope_ref[...]).astype(bf16)
    bias_ref[...] = jnp.sum(gu.astype(f32), axis=1, keepdims=True)
    g_ref[0] = gu
    up = jnp.concatenate([rows_by_inputs(up_ref, b) for b in range(2)], axis=0)
    part = mm(up, gu, TN)

    @pl.when(g == 0)
    def _():
        acc[...] = part

    @pl.when(g > 0)
    def _():
        acc[...] += part

    @pl.when(g == 3)
    def _():
        split_cores(core_ref, acc[...], keep_ref, send_ref)


def run_ffn_back(w, core, low, slope):
    keep, send, bias, grads = call(
        ffn_back_kernel,
        (4,),
        [
            scalar(core),
            (w_up_spec(w.up_at), w.up),
            (w_down_spec(w.down_at), w.down),
            whole(low),
            (by_step(512, 256), slope),
        ],
        [
            *PAIR,
            (by_step(512, 1), jax.ShapeDtypeStruct((2048, 1), f32)),
            (pl.BlockSpec((1, 512, 256), lambda g: (g, 0, 0)), jax.ShapeDtypeStruct((4, 512, 256), bf16)),
        ],
        [pltpu.VMEM((D, 256), f32)],
        flops=4 * 2048 * 1024 * 256,
        moved=14 << 20,
    )
    return (keep, send), grads, bias


def wide(refs, top, rows):
    return jnp.concatenate([ref[top : top + rows] for ref in refs], axis=1)


def from_chips(src_ref, refs):
    if len(refs) == 4:
        return jnp.concatenate([ref[...] for ref in refs], axis=1)
    return jnp.concatenate([refs[0][src_ref[i]] for i in range(4)], axis=1)


def down_grad_kernel(*refs):
    o_ref = refs[-1]
    gd = mm(wide(refs[:4], 0, 256), jnp.concatenate([ref[0] for ref in refs[4:8]], axis=1), NT).astype(bf16)
    for z in range(4):
        for j in range(4):
            o_ref[0, z, j * 64 : (j + 1) * 64, :] = gd[z * 64 : (z + 1) * 64, j * 128 : (j + 1) * 128]


def run_down_grad(l, low, active):
    return call(
        down_grad_kernel,
        (4,),
        [*[(by_step(256, 256), v) for v in low], *[(pl.BlockSpec((1, 512, 256), lambda g: (l, 0, 0)), v) for v in active]],
        [(pl.BlockSpec((1, 4, 256, 128), lambda g: (g, 0, 0, 0)), jax.ShapeDtypeStruct((4, 4, 256, 128), bf16))],
        flops=2 * 1024 * 1024 * 512,
        moved=6 << 20,
    )[0]


def up_grad_kernel(src_ref, *refs):
    o_ref = refs[-1]
    gu = mm(wide(refs[:4], 0, 512), from_chips(src_ref, refs[4:-1]), NT).astype(bf16)
    for a in range(2):
        for b in range(2):
            o_ref[0, a * 2 + b] = gu[b * 256 : (b + 1) * 256, a * 128 : (a + 1) * 128]


def attend_grad_kernel(top, src_ref, *refs):
    o_ref = refs[-1]
    g_refs, others = refs[:4], refs[4:-1]
    half = len(others) // 2
    go = mm(wide(g_refs, top, 256), from_chips(src_ref, others[:half]), NT).astype(bf16)
    gq = mm(wide(g_refs, top + 256, 384), from_chips(src_ref, others[half:]), NT).astype(bf16)
    for a in range(2):
        for b in range(2):
            z = a * 2 + b
            for j in range(3):
                at = j * 128 + b * 64
                o_ref[0, z, j * 64 : (j + 1) * 64, :] = gq[at : at + 64, a * 128 : (a + 1) * 128]
            o_ref[0, z, 192:256, :] = go[z * 64 : (z + 1) * 64]


def inputs_specs(inputs, rows, base):
    if isinstance(inputs, list):
        return [(pl.BlockSpec((rows, 256), lambda g: (base + g, 0)), v) for v in inputs]
    return [(pl.BlockSpec((4, rows, 256), lambda g: (0, base + g, 0)), inputs)]


def run_grad(kernel, src, arrived, inputs, *specs):
    return call(
        kernel,
        (4,),
        [
            scalar(src),
            *[whole(v) for v in arrived],
            *[one for spec in specs for one in inputs_specs(inputs, *spec)],
        ],
        [(pl.BlockSpec((1, 4, 256, 128), lambda g: (g, 0, 0, 0)), jax.ShapeDtypeStruct((4, 4, 256, 128), bf16))],
        flops=2 * 1024 * 1024 * 512,
        moved=6 << 20,
    )[0]


def run_up_grad(src, arrived, inputs):
    return run_grad(up_grad_kernel, src, arrived, inputs, (256, 0))


def run_attend_grad(top, src, arrived, inputs):
    return run_grad(partial(attend_grad_kernel, top), src, arrived, inputs, (128, 8), (256, 6))


def out_back_kernel(w_ref, low_ref, o_ref):
    r = mm(out_block(w_ref), low_ref[...], TN).astype(bf16)
    for s in range(2):
        for h in range(4):
            o_ref[s * 4 + h] = r[h * 128 : (h + 1) * 128, s * 128 : (s + 1) * 128]


def run_out_back(w, low):
    return call(
        out_back_kernel,
        (1,),
        [(w_out_spec(w.qo_at), w.qo), whole(low)],
        [out_whole((8, 128, 128), bf16)],
        flops=2 * 1024 * 512 * 256,
        moved=2 << 20,
    )[0]


def qkv_back_kernel(core_ref, w_ref, gq_ref, low_ref, keep_ref, send_ref, g_ref, bias_ref, acc):
    g = pl.program_id(0)
    both = jnp.concatenate([gq_ref[0, 0], gq_ref[1, 0]], axis=1)
    g_ref[0, 0:256] = low_ref[...]
    g_ref[0, 256:640] = both
    part = None
    for b in range(2):
        gq = jnp.concatenate([both[j * 128 + b * 64 : j * 128 + b * 64 + 64] for j in range(3)], axis=0)
        bias_ref[0, b] = jnp.sum(gq.astype(f32), axis=1, keepdims=True)
        term = mm(rows_by_inputs(w_ref, b, 192), gq, TN)
        part = term if part is None else part + term

    @pl.when(g == 0)
    def _():
        acc[...] = part

    @pl.when(g > 0)
    def _():
        acc[...] += part

    @pl.when(g == 3)
    def _():
        split_cores(core_ref, acc[...], keep_ref, send_ref)


def run_qkv_back(w, core, arrived, low):
    keep, send, grads, bias = call(
        qkv_back_kernel,
        (4,),
        [
            scalar(core),
            (w_qkv_spec(w.qo_at), w.qo),
            (pl.BlockSpec((2, 1, 384, 128), lambda g: (0, g, 0, 0)), arrived.reshape(2, 4, 384, 128)),
            (by_step(256, 256), low),
        ],
        [
            *PAIR,
            (pl.BlockSpec((1, 640, 256), lambda g: (g, 0, 0)), jax.ShapeDtypeStruct((4, 640, 256), bf16)),
            (pl.BlockSpec((1, 2, 192, 1), lambda g: (g, 0, 0, 0)), jax.ShapeDtypeStruct((4, 2, 192, 1), f32)),
        ],
        [pltpu.VMEM((D, 256), f32)],
        flops=2 * 1536 * 1024 * 256,
        moved=7 << 20,
    )
    return (keep, send), grads, bias


FACTOR = HEAD ** (-0.5)
STEP = 256


def join_tokens(ref, top):
    return jnp.concatenate([ref[c, top : top + HEAD] for c in range(8)], axis=1)


def attend_kernel(p_ref, o_ref, log_ref):
    for h in range(2):
        q = join_tokens(p_ref, h * 64)
        k = join_tokens(p_ref, 128 + h * 64)
        v = join_tokens(p_ref, 256 + h * 64)
        for c in range(SEQ_LEN // STEP):
            scores = mm(k, q[:, c * STEP : (c + 1) * STEP], TN) * FACTOR
            highest = jnp.max(scores, axis=0, keepdims=True)
            exps = jnp.exp(scores - highest)
            total = jnp.sum(exps, axis=0, keepdims=True)
            low = (exps * (1.0 / total)).astype(bf16)
            out = mm(v, low, NN).astype(bf16)
            log_ref[h : h + 1, c * STEP : (c + 1) * STEP] = highest + jnp.log(total)
            for n in range(STEP // 128):
                o_ref[c * (STEP // 128) + n, h * 64 : h * 64 + 64, :] = out[:, n * 128 : (n + 1) * 128]


def run_attend(packed):
    return call(
        attend_kernel,
        (1,),
        [whole(packed)],
        [out_whole((8, 128, 128), bf16), out_whole((2, SEQ_LEN), f32)],
        flops=8 * 1024 * 1024 * 128,
        moved=1 << 20,
    )


def attend_back_kernel(p_ref, b_ref, log_ref, o_ref):
    for h in range(2):
        q = join_tokens(p_ref, h * 64)
        k = join_tokens(p_ref, 128 + h * 64)
        v = join_tokens(p_ref, 256 + h * 64)
        gb = join_tokens(b_ref, h * 64)
        gk = gv = None
        for c in range(SEQ_LEN // STEP):
            cols = slice(c * STEP, (c + 1) * STEP)
            qc, gc = q[:, cols], gb[:, cols]
            probs = jnp.exp(mm(k, qc, TN) * FACTOR - log_ref[h : h + 1, cols])
            gp = mm(v, gc, TN)
            row = jnp.sum(probs * gp, axis=0, keepdims=True)
            ds = (probs * (gp - row)).astype(bf16)
            tv = mm(gc, probs.astype(bf16), NT)
            tk = mm(qc, ds, NT)
            gv = tv if gv is None else gv + tv
            gk = tk if gk is None else gk + tk
            gq = (mm(k, ds, NN) * FACTOR).astype(bf16)
            for n in range(STEP // 128):
                o_ref[c * (STEP // 128) + n, h * 64 : h * 64 + 64, :] = gq[:, n * 128 : (n + 1) * 128]
        gk = (gk * FACTOR).astype(bf16)
        gv = gv.astype(bf16)
        for c in range(8):
            o_ref[c, 128 + h * 64 : 192 + h * 64, :] = gk[:, c * 128 : (c + 1) * 128]
            o_ref[c, 256 + h * 64 : 320 + h * 64, :] = gv[:, c * 128 : (c + 1) * 128]


def run_attend_back(packed, grad, log):
    return call(
        attend_back_kernel,
        (1,),
        [whole(packed), whole(grad), whole(log)],
        [out_whole((8, 384, 128), bf16)],
        flops=20 * 1024 * 1024 * 128,
        moved=2 << 20,
    )[0]


def seq_swap(values):
    return lax.all_to_all(values, SEQ, 0, 0, tiled=True)


def norm_forward(summed, gain, shift):
    centre = jnp.mean(summed, axis=0, keepdims=True)
    centred = summed - centre
    variance = jnp.mean(centred * centred, axis=0, keepdims=True)
    scaled = lax.rsqrt(variance + epsilon)
    normed = centred * scaled
    return normed * gain[:, None] + shift[:, None], normed, scaled


def norm_backward(incoming, normed, scaled, gain):
    grad_norm = incoming * gain[:, None]
    plain = jnp.mean(grad_norm, axis=0, keepdims=True)
    cross = jnp.mean(grad_norm * normed, axis=0, keepdims=True)
    return scaled * (grad_norm - plain - normed * cross)


def on_device(
    tokens,
    w_qkv,
    bias_qv,
    w_out,
    bias_out,
    gain_attn,
    shift_attn,
    w_up,
    bias_up,
    w_down,
    bias_down,
    gain_ffn,
    shift_ffn,
    cotangent,
):
    core = lax.axis_index(CORE)
    here = core.astype(jnp.int32).reshape(1)
    src = jnp.stack([(lax.axis_index(X) - i) % 4 for i in SHIFTS]).astype(jnp.int32)
    traded = trade(
        jnp.concatenate([w_qkv.reshape(LAYERS, 192, 128), w_up.reshape(LAYERS, 256, 128)], axis=1)
    )
    pack = jnp.concatenate(
        [
            traded[:, :192],
            w_out,
            traded[:, 192:],
            w_down.reshape(LAYERS, 64, 4, 128).transpose(0, 2, 1, 3).reshape(LAYERS, 256, 128),
        ],
        axis=1,
    )
    head = jnp.concatenate([pack[0], pack[1, :256]], axis=0)
    head = lax.all_gather(head, CHIPS, axis=0, tiled=False).reshape(4, 4, 2, 2, 1024, 128)
    tail = lax.all_gather(pack[1, 256:], CHIPS, axis=0, tiled=False).reshape(4, 4, 2, 2, 512, 128)
    weights = (Weights(head, head, head, 0, 1, 2), Weights(head, tail, tail, 3, 0, 1))

    small = jnp.concatenate(
        [
            v.reshape(-1)
            for v in (bias_qv, bias_out, gain_attn, shift_attn, bias_down, gain_ffn, shift_ffn, bias_up)
        ]
    )
    small = lax.all_to_all(
        jnp.broadcast_to(small[None], (16, small.shape[0])), COL, 0, 0, tiled=True
    )
    b_qv = small[:, :256].reshape(4, 2, 2, LAYERS, 2, 64)
    b_qv = pick(b_qv, core, 1).transpose(2, 0, 1, 3, 4)
    b_qkv = jnp.stack([b_qv[:, :, :, 0], jnp.zeros_like(b_qv[:, :, :, 0]), b_qv[:, :, :, 1]], axis=3)
    b_qkv = jnp.broadcast_to(b_qkv.reshape(LAYERS, 4, 2, 192, 1), (LAYERS, 4, 2, 192, 128))
    features = small[:, 256:1024].reshape(16, 6, LAYERS, 64).transpose(1, 2, 0, 3).reshape(6, LAYERS, D)
    b_out, g_attn, s_attn, b_down, g_ffn, s_ffn = features
    b_up = small[:, 1024:].reshape(4, 2, 2, LAYERS, 256)
    b_up = pick(b_up, core, 1).transpose(2, 0, 1, 3)
    b_up = jnp.broadcast_to(b_up[..., None], (LAYERS, 4, 2, 256, 128))

    stream = lax.all_to_all(tokens, COL, 1, 0, tiled=True).astype(f32)
    back = lax.all_to_all(cotangent, COL, 1, 0, tiled=True).astype(f32)
    stream, back = lax.optimization_barrier((stream, back))
    stored = []
    for l in range(LAYERS):
        seen = core_gather(stream.astype(bf16))
        packed = seq_swap(run_qkv(weights[l], seen, b_qkv[l]))
        mixed, log = run_attend(packed)
        pair, blended = run_out(weights[l], here, seq_swap(mixed))
        attn_out = core_add(pair) + b_out[l][:, None]
        first, n_attn, i_attn = norm_forward(stream + attn_out, g_attn[l], s_attn[l])
        first_seen = core_gather(first.astype(bf16))
        pair, active, slope = run_ffn(weights[l], here, first_seen, b_up[l])
        lower = core_add(pair) + b_down[l][:, None]
        stream, n_ffn, i_ffn = norm_forward(first + lower, g_ffn[l], s_ffn[l])
        inputs = jnp.concatenate([first_seen, blended, seen], axis=0)
        inputs = lax.all_gather(inputs, X, axis=0, tiled=False)
        stored.append((inputs, active, packed, log, n_attn, i_attn, slope, n_ffn, i_ffn))
    result = stream.astype(bf16)
    active = jnp.stack([kept[1].reshape(4, 512, 256) for kept in stored], axis=1)
    active = exchange(active, Y)

    minor = [None] * LAYERS
    for l in reversed(range(LAYERS)):
        (inputs, _, packed, log, n_attn, i_attn, slope, n_ffn, i_ffn) = stored[l]
        grad_sum = norm_backward(back, n_ffn, i_ffn, g_ffn[l])
        p_gain_ffn = jnp.sum(back * n_ffn, axis=1)
        p_shift_ffn = jnp.sum(back, axis=1)
        low = grad_sum.astype(bf16)
        p_down = jnp.sum(low.astype(f32), axis=1)
        low = core_gather(low)
        g_down = everyone(low, Y)
        pair, send_up, p_up = run_ffn_back(weights[l], here, low, slope)
        if l == 0:
            g_up = exchange(send_up, X)
        if l == 0:
            late = after(late, send_up)
            downs = jnp.stack(
                [run_down_grad(0, g_down, active), run_down_grad(1, late[0], active)], axis=2
            )
            rest = jnp.concatenate(
                [run_up_grad(src, late[1], late[2]), run_attend_grad(512, src, late[1], late[2])], axis=2
            )
        grad_first = core_add(pair) + grad_sum
        p_gain_attn = jnp.sum(grad_first * n_attn, axis=1)
        p_shift_attn = jnp.sum(grad_first, axis=1)
        grad_total = norm_backward(grad_first, n_attn, i_attn, g_attn[l])
        low = grad_total.astype(bf16)
        p_out = jnp.sum(low.astype(f32), axis=1)
        low = core_gather(low)
        grad_blended = seq_swap(run_out_back(weights[l], low))
        grad_qkv = seq_swap(run_attend_back(packed, grad_blended, log))
        if l == 0:
            low, downs, rest, up_0 = lax.optimization_barrier(
                (low, downs, rest, run_up_grad(src, g_up, inputs))
            )
            rest = lax.psum_scatter(rest, Y, scatter_dimension=0)
            downs = reduce_stage(downs.reshape(16, 512, 128), COL)
        pair, send_qo, p_qkv = run_qkv_back(weights[l], here, grad_qkv, low)
        if l == 1:
            late = (g_down, exchange(jnp.concatenate([send_up, send_qo], axis=1), X), inputs)
        else:
            send_qo = after(send_qo, downs)
            g_qo = exchange(send_qo, X)
            first = jnp.concatenate(
                [up_0, run_attend_grad(0, src, g_qo, inputs)], axis=2
            )
            pair = after(pair, first)
            rest = lax.psum_scatter(after(rest, first), Z, scatter_dimension=0)
            first = reduce_stage(first.reshape(16, 512, 128), ("y",) + Z)
        back = core_add(pair) + grad_total
        minor[l] = (p_qkv, p_out, p_gain_attn, p_shift_attn, p_down, p_gain_ffn, p_shift_ffn, p_up)
    rest = after(rest, send_qo).astype(f32)
    sums = ((downs[:256], first[:256], first[256:]), (downs[256:], rest[:256], rest[256:]))
    swapped = trade(
        jnp.stack([jnp.concatenate([q[:192], u], axis=0) for _, u, q in sums]).astype(bf16)
    ).astype(f32)
    big = [
        (
            swapped[l, :192].reshape(3, 64, 128),
            sums[l][2][192:],
            swapped[l, 192:],
            sums[l][0].reshape(4, 64, 128).transpose(1, 0, 2).reshape(64, 512),
        )
        for l in range(LAYERS)
    ]
    mine = (jnp.arange(2) == core).astype(f32)
    qv = jnp.stack([m[0].reshape(4, 2, 3, 64)[:, :, ::2] for m in minor])
    qv = qv.transpose(1, 2, 0, 3, 4)
    qv = (qv[:, None] * mine[None, :, None, None, None, None]).reshape(16, 256)
    up = jnp.stack([m[7] for m in minor]).reshape(LAYERS, 4, 2, 256).transpose(1, 2, 0, 3)
    up = (up[:, None] * mine[None, :, None, None, None]).reshape(16, 512)
    feats = jnp.stack([jnp.stack([m[i] for m in minor]) for i in range(1, 7)])
    feats = feats.reshape(6, LAYERS, 16, 64).transpose(2, 0, 1, 3).reshape(16, 768)
    sums = jnp.concatenate([qv, feats, up], axis=1).reshape(16, 12, 128)
    high = sums.astype(bf16)
    low = (sums - high.astype(f32)).astype(bf16)
    send = jnp.concatenate([result.reshape(16, 64, 128), back.astype(bf16).reshape(16, 64, 128), high, low], axis=1)
    got = lax.all_to_all(send, COL, 0, 0, tiled=True)
    result = got[:, :64].transpose(1, 0, 2).reshape(64, 2048)
    grad_tokens = got[:, 64:128].astype(f32).transpose(1, 0, 2).reshape(64, 2048)
    sums2 = jnp.sum(got[:, 128:140].astype(f32), axis=0) + jnp.sum(got[:, 140:].astype(f32), axis=0)
    sums2 = sum_axis(sums2, Y)
    sums2 = sums2 + lax.ppermute(sums2, CORE, [(0, 1), (1, 0)])
    flat = sums2.reshape(1536)
    o_qv = flat[:256].reshape(LAYERS, 2, 64)
    o_out, o_gain_attn, o_shift_attn, o_down, o_gain_ffn, o_shift_ffn = flat[256:1024].reshape(6, LAYERS, 64)
    o_up = flat[1024:].reshape(LAYERS, 256)
    gw_qkv, gw_out, gw_up, gw_down = [jnp.stack([b[i] for b in big]) for i in range(4)]
    return (
        result,
        grad_tokens,
        gw_qkv,
        o_qv,
        gw_out,
        o_out,
        o_gain_attn,
        o_shift_attn,
        gw_up,
        o_up,
        gw_down,
        o_down,
        o_gain_ffn,
        o_shift_ffn,
    )


def solution(mesh):
    fine = Mesh(mesh.devices.reshape(4, 2, 2, 2, 2, 2), ("y", "k", "xh", "xl", "zh", "zl"))
    row = ("y", "k")
    col = COL
    in_specs = (
        P(col, row),
        P(None, None, col, row),
        P(None, None, col),
        P(None, col, row),
        P(None, col),
        P(None, col),
        P(None, col),
        P(None, col, row),
        P(None, col),
        P(None, col, row),
        P(None, col),
        P(None, col),
        P(None, col),
        P(col, row),
    )
    out_specs = (
        P(col, row),
        P(col, row),
        P(None, None, col, row),
        P(None, None, col),
        P(None, col, row),
        P(None, col),
        P(None, col),
        P(None, col),
        P(None, col, row),
        P(None, col),
        P(None, col, row),
        P(None, col),
        P(None, col),
        P(None, col),
    )
    return jax.shard_map(
        on_device, mesh=fine, in_specs=in_specs, out_specs=out_specs, check_vma=False
    )
```
